128 devices in a mesh: seq: 32 (over y_lo, x, z), fsdp: 4 (over y_hi, core).
Axes of the slice: x: 4, y: 4 (y_hi: 2, y_lo: 2; y = y_hi * 2 + y_lo), z: 4, core: 2. Of those that a mesh axis runs over, the one named last changes fastest.
Arguments:
- tokens: bfloat16 [4, 4096, 1024], P('fsdp', 'seq'), may hold values from -6 to 6
- query_weight: bfloat16 [1024, 1024], P('fsdp'), may hold values from -0.1875 to 0.1875
- key_weight: bfloat16 [1024, 1024], P('fsdp'), may hold values from -0.1875 to 0.1875
- value_weight: bfloat16 [1024, 1024], P('fsdp'), may hold values from -0.1875 to 0.1875
- output_weight: bfloat16 [1024, 1024], P('fsdp'), may hold values from -1.5 to 1.5
- expand_weight: bfloat16 [1024, 4096], P(None, 'fsdp'), may hold values from -0.1875 to 0.1875
- contract_weight: bfloat16 [4096, 1024], P('fsdp'), may hold values from -0.09375 to 0.09375
- query_bias: bfloat16 [1024], P('fsdp'), may hold values from -3 to 3
- value_bias: bfloat16 [1024], P('fsdp'), may hold values from -0.59765625 to 0.59765625
- output_bias: bfloat16 [1024], P('fsdp'), may hold values from -2 to 2
- expand_bias: bfloat16 [4096], P('fsdp'), may hold values from -3 to 3
- contract_bias: bfloat16 [1024], P('fsdp'), may hold values from -2 to 2
- first_gain: bfloat16 [1024], P('fsdp'), may hold values from 0.5 to 1.5
- first_shift: bfloat16 [1024], P('fsdp'), may hold values from -2 to 2
- second_gain: bfloat16 [1024], P('fsdp'), may hold values from 0.5 to 1.5
- second_shift: bfloat16 [1024], P('fsdp'), may hold values from -2 to 2
- cotangent: bfloat16 [4, 4096, 1024], P('fsdp', 'seq'), may hold values from -6 to 6
Outputs:
- block_output: bfloat16 [4, 4096, 1024], P('fsdp', 'seq')
- input_grad: bfloat16 [4, 4096, 1024], P('fsdp', 'seq')
- grad_query_weight: float32 [1024, 1024], P('fsdp')
- grad_key_weight: float32 [1024, 1024], P('fsdp')
- grad_value_weight: float32 [1024, 1024], P('fsdp')
- grad_output_weight: float32 [1024, 1024], P('fsdp')
- grad_expand_weight: float32 [1024, 4096], P(None, 'fsdp')
- grad_contract_weight: float32 [4096, 1024], P('fsdp')
- grad_query_bias: float32 [1024], P('fsdp')
- grad_value_bias: float32 [1024], P('fsdp')
- grad_output_bias: float32 [1024], P('fsdp')
- grad_expand_bias: float32 [4096], P('fsdp')
- grad_contract_bias: float32 [1024], P('fsdp')
- grad_first_gain: float32 [1024], P('fsdp')
- grad_first_shift: float32 [1024], P('fsdp')
- grad_second_gain: float32 [1024], P('fsdp')
- grad_second_shift: float32 [1024], P('fsdp')
The draws below stay inside these ranges and needn't reach their ends.
All inputs are finite; a program needn't handle non-finite values.
Results may differ from the reference program's by a relative error of at most 0.03.
Values may be sent and summed in bfloat16 or wider, within the bound.
A program may use at most 192 MiB of HBM per device.

```python
import jax
import jax.numpy as jnp
from jax import lax

D = 1024
HEADS = 16
FF = 4096
TOK_DEV = 128
SEQ_LEN = 4096
SEQS = 4


def shard_levels(own_key, shape, split, low, top_value):
    def one(dim, parts):
        steps = jax.random.uniform(jax.random.fold_in(jax.random.fold_in(own_key, 6), dim), (parts,), jnp.float32, low / len(split), top_value / len(split))
        return jnp.repeat(jnp.exp(steps), shape[dim] // parts).reshape((-1,) + (1,) * (len(shape) - dim - 1))

    loudness = one(*split[0])
    for cut in split[1:]:
        loudness = loudness * one(*cut)
    return loudness


def gaussian(own_key, dims, scale, reach, shards=(), kind=jnp.bfloat16):
    values = jax.random.normal(own_key, dims, jnp.float32) * scale
    if len(shards) > 0:
        values = shard_levels(own_key, dims, shards, -0.22, 0.18) * values
    return jnp.clip(values, min=-reach, max=reach).astype(kind)


def setup_inputs(seed: int = 0) -> dict:
    keys = jax.random.split(jax.random.key(seed), 18)
    return {
        "tokens": gaussian(keys[0], (SEQS, SEQ_LEN, D), 1.0, 6.0, ((0, 4), (1, 32))),
        "query_weight": gaussian(keys[1], (D, D), D ** -0.5, 0.1875, ((0, 4),)),
        "key_weight": gaussian(keys[2], (D, D), D ** -0.5, 0.1875, ((0, 4),)),
        "value_weight": gaussian(keys[3], (D, D), D ** -0.5, 0.1875, ((0, 4),)),
        "output_weight": gaussian(keys[4], (D, D), (D // 64) ** -0.5, 1.5, ((0, 4),)),
        "expand_weight": gaussian(keys[5], (D, FF), D ** -0.5, 0.1875, ((1, 4),)),
        "contract_weight": gaussian(keys[6], (FF, D), FF ** -0.5, 0.09375, ((0, 4),)),
        "query_bias": gaussian(keys[7], (D,), 0.5, 3.0, ((0, 4),)),
        "value_bias": gaussian(keys[8], (D,), 0.1, 0.59765625, ((0, 4),)),
        "output_bias": gaussian(keys[9], (D,), 0.3, 2.0, ((0, 4),)),
        "expand_bias": gaussian(keys[10], (FF,), 0.5, 3.0, ((0, 4),)),
        "contract_bias": gaussian(keys[11], (D,), 0.3, 2.0, ((0, 4),)),
        "first_gain": jnp.clip(1.0 + 0.1 * jax.random.normal(keys[12], (D,), jnp.float32), 0.5, 1.5).astype(jnp.bfloat16),
        "first_shift": gaussian(keys[13], (D,), 0.3, 2.0, ((0, 4),)),
        "second_gain": jnp.clip(1.0 + 0.1 * jax.random.normal(keys[14], (D,), jnp.float32), 0.5, 1.5).astype(jnp.bfloat16),
        "second_shift": gaussian(keys[15], (D,), 0.3, 2.0, ((0, 4),)),
        "cotangent": gaussian(keys[16], (SEQS, SEQ_LEN, D), 1.0, 6.0, ((0, 4), (1, 32))),
    }


@jax.custom_vjp
def low(v):
    return lax.optimization_barrier(v.astype(jnp.bfloat16)).astype(jnp.float32)

@jax.custom_vjp
def low_back(v):
    return v

def low_keep(v):
    return (low(v), None)

def low_pass(kept, grad):
    return (grad,)

def back_keep(v):
    return (v, None)

def back_low(kept, grad):
    return (low(grad),)
low.defvjp(low_keep, low_pass)
low_back.defvjp(back_keep, back_low)

def rounded_both(values):
    return low(low_back(values))

def matmul(left, right):
    return jnp.dot(left, right, precision=lax.Precision.HIGHEST, preferred_element_type=jnp.float32)

def norm_layer(values, gain, shift):
    mean = lax.optimization_barrier(jnp.mean(values, axis=-1, keepdims=True))
    centered = values - mean
    variance = lax.optimization_barrier(jnp.mean(centered * centered, axis=-1, keepdims=True))
    return centered * lax.rsqrt(variance + 1e-05) * gain + shift

def gelu_tanh(values):
    return 0.5 * values * (1.0 + jnp.tanh(0.7978845608028654 * (values + 0.044715 * values * values * values)))

def dealt_place():
    rows = jnp.arange(SEQ_LEN, dtype=jnp.int32)
    device = rows // TOK_DEV
    inner = rows % TOK_DEV
    half = TOK_DEV // 2
    return jnp.where(inner < half, device * half + inner, SEQ_LEN - (device + 2) * half + inner).astype(jnp.int32)

def layer(params, rows):
    w_query, w_key, w_value, w_output, w_expand, w_contract, b_query, b_value, b_output, b_expand, b_contract, gain_one, shift_one, gain_two, shift_two = params
    seq_len = rows.shape[0]
    width = rows.shape[1]
    head_dim = width // HEADS
    place = dealt_place()
    first_in = low(norm_layer(rows, gain_one, shift_one))
    query = rounded_both(matmul(first_in, w_query) + b_query)
    key = rounded_both(matmul(first_in, w_key))
    value = rounded_both(matmul(first_in, w_value) + b_value)
    key_heads = key.reshape(seq_len, HEADS, head_dim)
    value_heads = value.reshape(seq_len, HEADS, head_dim)
    span = min(512, seq_len)

    def attend(pieces):
        query_block, place_block = pieces
        query_heads = query_block.reshape(span, HEADS, head_dim)
        scores = jnp.einsum('qhd,khd->hqk', query_heads, key_heads, precision=lax.Precision.HIGHEST) * 0.125
        scores = low_back(scores)
        visible = place_block[:, None] >= place[None, :]
        scores = jnp.where(visible[None], scores, -1e+30)
        top = lax.optimization_barrier(jnp.max(scores, axis=-1, keepdims=True))
        expo = jnp.exp(scores - top)
        probs = expo / lax.optimization_barrier(jnp.sum(expo, axis=-1, keepdims=True))
        out = jnp.einsum('hqk,khd->qhd', low(probs), value_heads, precision=lax.Precision.HIGHEST)
        return out.reshape(span, width)
    blocks = seq_len // span
    mixed = lax.map(jax.checkpoint(attend), (query.reshape(blocks, span, width), place.reshape(blocks, span)))
    mixed = rounded_both(mixed.reshape(seq_len, width))
    branch = low_back(matmul(mixed, w_output) + b_output)
    resid = rows + branch
    second_in = low(norm_layer(resid, gain_two, shift_two))
    pre = low_back(matmul(second_in, w_expand) + b_expand)
    activated = low(gelu_tanh(pre))
    ffn_out = low_back(matmul(activated, w_contract) + b_contract)
    return resid + ffn_out

def reference(tokens, query_weight, key_weight, value_weight, output_weight, expand_weight, contract_weight, query_bias, value_bias, output_bias, expand_bias, contract_bias, first_gain, first_shift, second_gain, second_shift, cotangent):
    params = tuple((p.astype(jnp.float32) for p in (query_weight, key_weight, value_weight, output_weight, expand_weight, contract_weight, query_bias, value_bias, output_bias, expand_bias, contract_bias, first_gain, first_shift, second_gain, second_shift)))

    def one_sequence(totals, pieces):
        rows, upstream = pieces
        result, pull = jax.vjp(layer, params, rows.astype(jnp.float32))
        grad_params, grad_rows = pull(upstream.astype(jnp.float32))
        totals = jax.tree.map(jnp.add, totals, grad_params)
        return (totals, (result.astype(jnp.bfloat16), grad_rows.astype(jnp.bfloat16)))
    zeros = tuple((jnp.zeros_like(p) for p in params))
    grads, (outputs, input_grads) = lax.scan(one_sequence, zeros, (tokens, cotangent))
    return (outputs, input_grads, grads[0], grads[1], grads[2], grads[3], grads[4], grads[5], grads[6], grads[7], grads[8], grads[9], grads[10], grads[11], grads[12], grads[13], grads[14])
```

```python
import functools

import jax
import jax.numpy as jnp
from jax import lax
from jax.experimental import pallas as pl
from jax.experimental.pallas import tpu as pltpu
from jax.sharding import PartitionSpec as P

MESH = pl.DeviceIdType.MESH
BF16 = jnp.bfloat16
F32 = jnp.float32
TILE = 512
HALF = 64
VMEM_LIMIT = 50 * 1024 * 1024


def matmul(left, right):
    return jnp.dot(left, right, preferred_element_type=F32)


def matmul_tn(left, right):
    return lax.dot_general(left, right, (((0,), (0,)), ((), ())), preferred_element_type=F32)


def matmul_nt(left, right):
    return lax.dot_general(left, right, (((1,), (1,)), ((), ())), preferred_element_type=F32)


def norm_parts(values, gain, shift):
    mean = jnp.mean(values, axis=-1, keepdims=True)
    centered = values - mean
    variance = jnp.mean(centered * centered, axis=-1, keepdims=True)
    inverse = lax.rsqrt(variance + 1e-05)
    normed = centered * inverse
    return (normed * gain + shift, normed, inverse)


def norm_back(grad, normed, inverse, gain):
    scaled = grad * gain
    return inverse * (
        scaled
        - jnp.mean(scaled, axis=-1, keepdims=True)
        - normed * jnp.mean(scaled * normed, axis=-1, keepdims=True)
    )


def gelu_both(values):
    square = values * values
    inner = jnp.tanh(0.7978845608028654 * (values + 0.044715 * square * values))
    value = 0.5 * values * (1.0 + inner)
    slope = 0.5 * (1.0 + inner) + 0.5 * values * (1.0 - inner * inner) * 0.7978845608028654 * (
        1.0 + 0.134145 * square
    )
    return value, slope


class Place:
    def __init__(self):
        self.seq = lax.axis_index("seq")
        self.shard = lax.axis_index("fsdp")
        self.layer = self.seq // 16
        self.spot = self.seq % 16
        self.team = (self.layer + self.shard // 2) % 2


class Team:
    size = 4

    def __init__(self, place):
        self.place = place
        self.me = place.shard

    def device(self, t):
        return {"seq": ((self.place.team + t // 2) % 2) * 16 + self.place.spot, "fsdp": t}


class Plane:
    size = 16

    def __init__(self, place):
        self.place = place
        self.me = place.spot

    def device(self, t):
        return {"seq": self.place.layer * 16 + t, "fsdp": self.place.shard}


class Line:
    size = 32

    def __init__(self, place):
        self.place = place
        self.me = place.seq

    def device(self, t):
        return {"seq": t, "fsdp": self.place.shard}


def spread(count, body):
    if count <= 4:
        for step in range(count):
            body(step)
    else:
        lax.fori_loop(0, count, lambda step, c: (body(step), c)[1], 0)


def query_half(place):
    return (place.layer + place.shard // 2 + place.spot // 8) % 2


def tile_place(half, tile):
    return half * 2 + tile if tile < 2 else 6 - 2 * half + tile - 2


def spread_rows(src_ref, out_ref, at_high, factor):
    lane = lax.broadcasted_iota(jnp.int32, (HALF, 128), 1)
    keep = (lane >= HALF) if at_high else (lane < HALF)
    for block in range(16):
        both = src_ref[block].astype(F32) * factor
        moved = pltpu.roll(both, HALF, 1)
        low, high = (moved, both) if at_high else (both, moved)
        out_ref[pl.ds(block * HALF, HALF), :] = jnp.where(keep, low, 0.0).astype(BF16)
        out_ref[pl.ds(1024 + (15 - block) * HALF, HALF), :] = jnp.where(keep, high, 0.0).astype(BF16)


def turn_rows(src_ref, out_ref, rows):
    for at in range(0, rows, TILE):
        out_ref[:, pl.ds(at, TILE)] = src_ref[pl.ds(at, TILE), :].astype(F32).T.astype(BF16)


def pack_rows(turned, out_ref, tile):
    empty = jnp.zeros_like(turned)
    if tile < 2:
        rows = jnp.concatenate([turned, empty], axis=0).T.astype(BF16)
        for part in range(8):
            out_ref[tile * 8 + part] = rows[part * HALF : (part + 1) * HALF]
    else:
        rows = jnp.concatenate([empty, turned], axis=0).T.astype(BF16)
        for part in range(8):
            block = 15 - ((tile - 2) * 8 + part)
            out_ref[block] = out_ref[block] + rows[part * HALF : (part + 1) * HALF]


def key_rows(kt):
    return pl.ds(pl.multiple_of(kt * TILE, TILE), TILE)


def hide_later(scores):
    key = lax.broadcasted_iota(jnp.int32, (TILE, TILE), 0)
    query = lax.broadcasted_iota(jnp.int32, (TILE, TILE), 1)
    return jnp.where(key <= query, scores, -1e30)


def stored_block(sender_team, spot, sequence):
    return ((sender_team + sequence // 2) % 2) * 16 + spot


def swap_heads(low, high):
    low, high = low.astype(F32), high.astype(F32)
    left = lax.broadcasted_iota(jnp.int32, low.shape, 1) < HALF
    one = jnp.where(left, low, pltpu.roll(high, HALF, 1))
    two = jnp.where(left, pltpu.roll(low, HALF, 1), high)
    return one.astype(BF16), two.astype(BF16)


def head_pieces(sequence, pair):
    low = pl.ds(sequence * 128, HALF)
    high = pl.ds(sequence * 128 + HALF, HALF)
    lanes = pl.ds(pair * 128, 128)
    return (low, lanes), (high, lanes), sequence * 4 + pair * 2


def pack_into(out_ref, src_ref):
    for sequence in range(4):
        for pair in range(2):
            low, high, at = head_pieces(sequence, pair)
            out_ref[at], out_ref[at + 1] = swap_heads(src_ref[low], src_ref[high])


def unpack_into(out_ref, src_ref):
    for sequence in range(4):
        for pair in range(2):
            low, high, at = head_pieces(sequence, pair)
            out_ref[low], out_ref[high] = swap_heads(src_ref[at], src_ref[at + 1])


def kv_block(ref, spot, low):
    rows = pl.ds(pl.multiple_of((spot // 4) * 128 + (0 if low else HALF), HALF), HALF)
    return ref.at[rows, pl.ds(pl.multiple_of((spot % 4) * 128, 128), 128)]


def kv_place(block, low):
    return pl.ds(pl.multiple_of((block if low else 63 - block) * HALF, HALF), HALF)


class Column:
    size = 4

    def __init__(self, place):
        self.place = place
        self.me = place.shard

    def device(self, t):
        return {"seq": self.place.seq, "fsdp": t}


class Cube:
    def __init__(self, place):
        x, z = place.spot // 4, place.spot % 4
        self.shard = place.shard
        self.bits = [(x + x // 2) % 2, x // 2, (z + z // 2) % 2, z // 2, place.layer]

        def at(x, z, layer):
            return layer * 16 + x * 4 + z

        self.partners = [
            at(x + 1 - 2 * (x % 2), z, place.layer),
            at(3 - x, z, place.layer),
            at(x, z + 1 - 2 * (z % 2), place.layer),
            at(x, 3 - z, place.layer),
            at(x, z, 1 - place.layer),
        ]

    def device(self, bit):
        return {"seq": self.partners[bit], "fsdp": self.shard}


class Part:
    def __init__(self, cube, index, rows, least):
        self.cube = cube
        self.order = [(index + s) % 5 for s in range(5)]
        row = 0
        self.sent, self.held, self.halves = [], [(0, rows)], []
        for bit in self.order:
            value = cube.bits[bit]
            self.halves.append(rows > least)
            if rows > least:
                rows //= 2
                self.sent.append((row + (1 - value) * rows, rows))
                row = row + value * rows
            else:
                self.sent.append((row, rows))
            self.held.append((row, rows))

    def view(self, ref, region):
        row, rows = region
        return ref.at[pl.ds(row if isinstance(row, int) else pl.multiple_of(row, 16), rows)]

    def stage(self, step):
        rows = self.sent[step][1]
        return (rows if self.halves[step] else 0, rows)


class Halving:
    def __init__(self, parts, buffers, stages, send_sem, recv_sem):
        self.parts, self.buffers, self.stages = parts, buffers, stages
        self.send_sem, self.recv_sem = send_sem, recv_sem

    def copy(self, k, step):
        part = self.parts[k]
        return pltpu.make_async_remote_copy(
            src_ref=part.view(self.buffers[k], part.sent[step]),
            dst_ref=part.view(self.stages[k], part.stage(step)),
            send_sem=self.send_sem.at[k, step],
            recv_sem=self.recv_sem.at[k, step],
            device_id=part.cube.device(part.order[step]),
            device_id_type=MESH,
        )

    def send(self, step, which=None):
        for k in which or range(len(self.parts)):
            self.copy(k, step).start()

    def add(self, step):
        for k, part in enumerate(self.parts):
            self.copy(k, step).wait_recv()
            if not part.halves[step]:
                self.copy(k, step).wait_send()
            mine = part.view(self.buffers[k], part.held[step + 1])
            other = part.view(self.stages[k], part.stage(step))
            rows = part.held[step + 1][1]

            def slab(at, c, mine=mine, other=other):
                here = pl.ds(pl.multiple_of(at * 16, 16), 16)
                mine[here, :] = (mine[here, :].astype(F32) + other[here, :].astype(F32)).astype(BF16)
                return c

            if rows == 16:
                slab(0, 0)
            else:
                lax.fori_loop(0, rows // 16, slab, 0)

    def finish(self):
        for k, part in enumerate(self.parts):
            for step in range(5):
                if part.halves[step]:
                    self.copy(k, step).wait_send()


class Doubling:
    def __init__(self, parts, buffers, send_sem, recv_sem):
        self.parts, self.buffers = parts, buffers
        self.send_sem, self.recv_sem = send_sem, recv_sem

    def copy(self, k, step):
        part = self.parts[k]
        view = part.view(self.buffers[k], part.held[step + 1])
        return pltpu.make_async_remote_copy(
            src_ref=view,
            dst_ref=view,
            send_sem=self.send_sem.at[k, step],
            recv_sem=self.recv_sem.at[k, step],
            device_id=part.cube.device(part.order[step]),
            device_id_type=MESH,
        )

    def landed(self, k, step):
        part = self.parts[k]
        view = part.view(self.buffers[k], part.sent[step])
        return pltpu.make_async_remote_copy(
            src_ref=view,
            dst_ref=view,
            send_sem=self.send_sem.at[k, step],
            recv_sem=self.recv_sem.at[k, step],
            device_id=part.cube.device(part.order[step]),
            device_id_type=MESH,
        )

    def send(self, step):
        for k in range(len(self.parts)):
            self.copy(k, step).start()

    def take(self, step):
        for k in range(len(self.parts)):
            self.landed(k, step).wait_recv()

    def finish(self):
        for k in range(len(self.parts)):
            for step in range(4):
                self.copy(k, step).wait_send()


def big_parts(cube):
    return [Part(cube, k, 512, 32) for k in range(5)]


def meet(groups):
    barrier = pltpu.get_barrier_semaphore()
    for grp in groups:

        def hello(step, grp=grp):
            pl.semaphore_signal(
                barrier, inc=1, device_id=grp.device((grp.me + 1 + step) % grp.size), device_id_type=MESH
            )

        spread(grp.size - 1, hello)
    pl.semaphore_wait(barrier, sum(grp.size - 1 for grp in groups))


class Swap:
    def __init__(self, group, src, dst, send_sem, recv_sem, local_sem):
        self.group, self.src, self.dst = group, src, dst
        self.send_sem, self.recv_sem, self.local_sem = send_sem, recv_sem, local_sem

    def copy(self, target):
        return pltpu.make_async_remote_copy(
            src_ref=self.src(target),
            dst_ref=self.dst(self.group.me, target),
            send_sem=self.send_sem.at[target],
            recv_sem=self.recv_sem.at[self.group.me],
            device_id=self.group.device(target),
            device_id_type=MESH,
        )

    def landed(self, sender):
        view = self.dst(sender, self.group.me)
        return pltpu.make_async_remote_copy(
            src_ref=view,
            dst_ref=view,
            send_sem=self.send_sem.at[sender],
            recv_sem=self.recv_sem.at[sender],
            device_id=self.group.device(sender),
            device_id_type=MESH,
        )

    def own(self):
        return pltpu.make_async_copy(
            self.src(self.group.me), self.dst(self.group.me, self.group.me), self.local_sem
        )

    def send(self, step):
        self.copy((self.group.me + 1 + step) % self.group.size).start()

    def take(self, step):
        self.landed((self.group.me + 1 + step) % self.group.size).wait_recv()

    def sent(self, step):
        self.copy((self.group.me + 1 + step) % self.group.size).wait_send()

    def send_all(self):
        spread(self.group.size - 1, self.send)
        self.own().start()

    def take_all(self):
        spread(self.group.size - 1, self.take)
        self.own().wait()

    def sent_all(self):
        spread(self.group.size - 1, self.sent)


def swap_sems(count):
    return [
        pltpu.SemaphoreType.DMA((count, 32)),
        pltpu.SemaphoreType.DMA((count, 32)),
        pltpu.SemaphoreType.DMA((count,)),
    ]


class Square:
    size = 4

    def __init__(self, place):
        self.place = place
        self.x, self.z = place.spot // 4, place.spot % 4
        self.me = ((self.x + self.x // 2) % 2) * 2 + (self.z + self.z // 2) % 2

    def device(self, t):
        x = 2 * (self.x // 2) + (t // 2 + self.x // 2) % 2
        z = 2 * (self.z // 2) + (t % 2 + self.z // 2) % 2
        return {"seq": self.place.layer * 16 + x * 4 + z, "fsdp": self.place.shard}


class Columns:
    def __init__(self, team, square, sources, out, sems):
        self.team, self.square, self.sources, self.out = team, square, sources, out
        self.near_send, self.near_recv, self.far_send, self.far_recv, self.pass_send, self.pass_recv, self.local = sems
        me = team.me
        self.me = me
        self.sibling = (me // 2) * 2 + 1 - me % 2
        across = (me + 2) % 4
        self.far = (across, (self.sibling + 2) % 4)

    def lanes(self, member):
        return pl.ds(pl.multiple_of(member * 256, 256), 256)

    def block(self, k, member):
        return self.out.at[k, self.lanes(member)]

    def quarter(self, k, member, spot):
        return self.out.at[k, pl.ds(pl.multiple_of(member * 256 + spot * 64, 64), 64)]

    def remote(self, src, dst, send_sem, recv_sem, device):
        return pltpu.make_async_remote_copy(
            src_ref=src, dst_ref=dst, send_sem=send_sem, recv_sem=recv_sem, device_id=device, device_id_type=MESH
        )

    def near(self, k, arriving=False):
        dst = self.block(k, self.sibling if arriving else self.me)
        src = dst if arriving else self.sources[k].at[:, self.lanes(self.sibling)]
        return self.remote(src, dst, self.near_send.at[k], self.near_recv.at[k], self.team.device(self.sibling))

    def far_copy(self, k, which, arriving=False):
        other = self.far[which]
        dst = self.quarter(k, other if arriving else self.me, self.square.me)
        rows = pl.ds(pl.multiple_of(self.square.me * 64, 64), 64)
        src = dst if arriving else self.sources[k].at[rows, self.lanes(other)]
        at = which * 3 + k
        return self.remote(src, dst, self.far_send.at[at], self.far_recv.at[at], self.team.device(other))

    def pass_copy(self, k, which, step, arriving=False):
        spot = (self.square.me + 1 + step) % 4
        view = self.quarter(k, self.far[which], spot if arriving else self.square.me)
        at = which * 3 + k
        return self.remote(
            view, view, self.pass_send.at[at, spot], self.pass_recv.at[at, spot if arriving else self.square.me],
            self.square.device(spot),
        )

    def own(self, k):
        return pltpu.make_async_copy(self.sources[k].at[:, self.lanes(self.me)], self.block(k, self.me), self.local.at[k])

    def send(self):
        for k in range(3):
            for which in range(2):
                self.far_copy(k, which).start()
        for k in range(3):
            self.near(k).start()
            self.own(k).start()

    def forward(self):
        for k in range(3):
            for which in range(2):
                self.far_copy(k, which, True).wait_recv()
                for step in range(3):
                    self.pass_copy(k, which, step).start()

    def take(self):
        for k in range(3):
            self.own(k).wait()
            self.near(k, True).wait_recv()
            for which in range(2):
                for step in range(3):
                    self.pass_copy(k, which, step, True).wait_recv()

    def sent(self):
        for k in range(3):
            self.near(k).wait_send()
            for which in range(2):
                self.far_copy(k, which).wait_send()
                for step in range(3):
                    self.pass_copy(k, which, step).wait_send()


COLUMN_SEMS = [
    *([pltpu.SemaphoreType.DMA((3,))] * 2),
    *([pltpu.SemaphoreType.DMA((6,))] * 2),
    *([pltpu.SemaphoreType.DMA((6, 4))] * 2),
    pltpu.SemaphoreType.DMA((3,)),
]


class Pair:
    size = 2

    def __init__(self, place):
        self.place = place
        self.me = place.layer

    def device(self, t):
        return {"seq": t * 16 + self.place.spot, "fsdp": self.place.shard}


class Fold:
    def __init__(self, team, part, near, far, send_sem, recv_sem):
        self.team, self.part, self.near, self.far = team, part, near, far
        self.send_sem, self.recv_sem = send_sem, recv_sem
        me = team.me
        self.me = me
        self.sibling = (me // 2) * 2 + 1 - me % 2
        self.across = (me + 2) % 4
        self.opposite = (self.sibling + 2) % 4

    def copy(self, k):
        if k < 2:
            src, dst, to = self.part.at[(self.opposite, self.sibling)[k]], self.near.at[k], self.sibling
        else:
            src, dst, to = self.part.at[self.across], self.far, self.across
        return pltpu.make_async_remote_copy(
            src_ref=src,
            dst_ref=dst,
            send_sem=self.send_sem.at[k],
            recv_sem=self.recv_sem.at[k],
            device_id=self.team.device(to),
            device_id_type=MESH,
        )

    def send(self, make):
        make(self.opposite)
        self.copy(0).start()
        make(self.across)
        self.copy(0).wait_recv()
        self.part[self.across] = (
            self.part[self.across].astype(F32) + self.near[0].astype(F32)
        ).astype(BF16)
        self.copy(2).start()
        make(self.sibling)
        self.copy(1).start()
        make(self.me)

    def total(self):
        self.copy(1).wait_recv()
        self.copy(2).wait_recv()
        return self.part[self.me].astype(F32) + self.near[1].astype(F32) + self.far[...].astype(F32)

    def sent(self):
        for k in range(3):
            self.copy(k).wait_send()


class Share:
    def __init__(self, team, out, own, send_sem, recv_sem):
        self.team, self.out, self.own = team, out, own
        self.send_sem, self.recv_sem = send_sem, recv_sem
        me = team.me
        self.me = me
        self.sibling = (me // 2) * 2 + 1 - me % 2
        self.across = (me + 2) % 4
        self.opposite = (self.sibling + 2) % 4

    def rows(self, k):
        return pl.ds((k % 2) * 64, 64)

    def copy(self, k):
        kind = k // 2
        src = self.own.at[self.rows(k)] if kind < 2 else self.out.at[self.across, self.rows(k)]
        block = self.me if kind < 2 else self.across
        return pltpu.make_async_remote_copy(
            src_ref=src,
            dst_ref=self.out.at[block, self.rows(k)],
            send_sem=self.send_sem.at[k],
            recv_sem=self.recv_sem.at[k],
            device_id=self.team.device(self.across if kind == 1 else self.sibling),
            device_id_type=MESH,
        )

    def landed(self, k):
        view = self.out.at[(self.sibling, self.across, self.opposite)[k // 2], self.rows(k)]
        return pltpu.make_async_remote_copy(
            src_ref=view,
            dst_ref=view,
            send_sem=self.send_sem.at[k],
            recv_sem=self.recv_sem.at[k],
            device_id=self.team.device(self.across if k // 2 == 1 else self.sibling),
            device_id_type=MESH,
        )

    def send(self):
        for k in (2, 3, 0, 1):
            self.copy(k).start()

    def forward(self):
        for k in (2, 3):
            self.landed(k).wait_recv()
            self.copy(k + 2).start()

    def take(self):
        for k in (0, 1, 4, 5):
            self.landed(k).wait_recv()

    def sent(self):
        for k in range(6):
            self.copy(k).wait_send()


TEAM_SEMS = [pltpu.SemaphoreType.DMA((6,)), pltpu.SemaphoreType.DMA((6,))]


def forward_kernel(
    x_ref, vec_ref, wo_ref, dy_ref, wq_ref, wk_ref, wv_ref,
    first_in_ref, mixed_ref, resid_ref, wide_ref, lse_ref, params_ref, q_out, kv_out, dy_out, second_out, w_out,
    x_all, vec_all, weights,
    q_mine, kv_mine, q_send, kv_send, rows, turned, kv_turned, mixed_mine, mixed_in, part, near, far, second,
    swap_send, swap_recv, swap_local, pass_send, pass_recv, save_sem,
    dy_send, dy_recv, fold_send, fold_recv, share_send, share_recv, x_send, x_recv, *column_sems,
):
    place = Place()
    plane, pair, team = Plane(place), Pair(place), Team(place)
    half = query_half(place)
    sequence = place.spot // 4

    def swap(k, group, src, dst):
        return Swap(group, src, dst, swap_send.at[k], swap_recv.at[k], swap_local.at[k])

    meet([plane, pair, team])
    dy = Share(team, dy_out, dy_ref, dy_send, dy_recv)
    dy_own = pltpu.make_async_copy(dy_ref, dy_out.at[team.me], save_sem.at[0])
    vec = swap(4, team, lambda t: vec_ref, lambda j, t: vec_all.at[j])
    columns = Columns(team, Square(place), (wq_ref, wk_ref, wv_ref), weights, column_sems)
    x = Share(team, x_all, x_ref, x_send, x_recv)
    vec.send_all()
    columns.send()
    x.send()
    dy_own.start()
    x_all[place.shard] = x_ref[...]
    columns.forward()
    x.forward()
    dy.send()
    vec.take_all()
    for t in range(4):
        params_ref[:, pl.ds(t * 256, 256)] = vec_all[t]
    x.take()
    columns.take()
    save_w = pltpu.make_async_copy(weights, w_out, save_sem.at[4])
    save_w.start()

    def kv_rows(layer, spot, seq, low):
        return kv_place(stored_block((layer + place.shard // 2) % 2, spot, seq), low)

    heads = [
        swap(
            k, plane,
            lambda t, k=k: kv_block(kv_send, t, k == 0),
            lambda j, t, k=k: kv_mine.at[kv_rows(place.layer, j, t // 4, k == 0)],
        )
        for k in range(2)
    ]
    heads.append(swap(2, plane, lambda t: q_send.at[t], lambda j, t: q_mine.at[j]))
    gain, shift = params_ref[pl.ds(0, 1), :], params_ref[pl.ds(1, 1), :]
    for turn in range(4):
        s = (sequence + 1 + turn) % 4
        normed = norm_parts(x_all[s].astype(F32), gain, shift)[0].astype(BF16)
        first_in_ref[pl.ds(pl.multiple_of(s * 128, 128), 128), :] = normed
        query = (matmul(normed, weights[0]) + vec_ref[pl.ds(6, 1), :]).astype(BF16)
        key = matmul(normed, weights[1]).astype(BF16)
        value = (matmul(normed, weights[2]) + vec_ref[pl.ds(7, 1), :]).astype(BF16)
        for two in range(2):
            lanes = slice(two * 128, two * 128 + 128)
            at = s * 4 + two * 2
            for part_of in range(2):
                cut = slice(part_of * HALF, part_of * HALF + HALF)
                one, other = swap_heads(key[cut, lanes], value[cut, lanes])
                down = pl.ds(pl.multiple_of(s * 128 + part_of * HALF, HALF), HALF)
                kv_send[down, two * 256 : two * 256 + 128] = one
                kv_send[down, two * 256 + 128 : two * 256 + 256] = other
            q_send[at], q_send[at + 1] = swap_heads(query[:HALF, lanes], query[HALF:, lanes])
        for head in range(4 if turn < 3 else 3):
            target = s * 4 + (place.spot + 1 + head) % 4
            for item in heads:
                item.copy(target).start()

    for item in heads:
        item.own().start()

    def pass_on(k, j):
        view = kv_mine.at[kv_rows(place.layer, j, sequence, k == 0)]
        return pltpu.make_async_remote_copy(
            src_ref=view,
            dst_ref=view,
            send_sem=pass_send.at[k, j],
            recv_sem=pass_recv.at[k, j],
            device_id=pair.device(1 - place.layer),
            device_id_type=MESH,
        )

    def passed(k, j):
        view = kv_mine.at[kv_rows(1 - place.layer, j, sequence, k == 0)]
        return pltpu.make_async_remote_copy(
            src_ref=view,
            dst_ref=view,
            send_sem=pass_send.at[k, j],
            recv_sem=pass_recv.at[k, j],
            device_id=pair.device(1 - place.layer),
            device_id_type=MESH,
        )

    for item in heads:
        item.own().wait()
    for k in range(2):
        pass_on(k, plane.me).start()

    def relay(step, c):
        j = (plane.me + 15 - step) % 16
        for k in range(2):
            heads[k].landed(j).wait_recv()
            pass_on(k, j).start()
        heads[2].landed(j).wait_recv()
        return c

    lax.fori_loop(0, 15, relay, 0)
    spread_rows(q_mine, rows, False, 0.125)
    turn_rows(rows, turned, 2048)

    def arrive(j, c):
        for k in range(2):
            passed(k, j).wait_recv()
        return c

    lax.fori_loop(0, 16, arrive, 0)
    saves = [
        pltpu.make_async_copy(q_mine, q_out, save_sem.at[1]),
        pltpu.make_async_copy(kv_mine, kv_out, save_sem.at[2]),
    ]
    for save in saves:
        save.start()
    dy.forward()
    turn_rows(kv_mine, kv_turned, 4096)
    mix = swap(3, plane, lambda t: mixed_mine.at[t], lambda j, t: mixed_in.at[j])
    for number, tile in enumerate((0, 3, 1, 2)):
        cols = pl.ds(tile * TILE, TILE)
        last = tile_place(half, tile)

        def step(kt, carry, masked):
            top, total, accum = carry
            scores = matmul(kv_mine[key_rows(kt), :], turned[:, cols])
            if masked:
                scores = hide_later(scores)
            new_top = jnp.maximum(top, jnp.max(scores, axis=0, keepdims=True))
            probs = jnp.exp(scores - new_top)
            fade = jnp.exp(top - new_top)
            total = total * fade + jnp.sum(probs, axis=0, keepdims=True)
            accum = accum * fade + matmul(kv_turned[HALF:, key_rows(kt)], probs.astype(BF16))
            return new_top, total, accum

        start = (
            jnp.full((1, TILE), -1e30, F32),
            jnp.zeros((1, TILE), F32),
            jnp.zeros((HALF, TILE), F32),
        )
        carry = lax.fori_loop(0, last, lambda kt, c: step(kt, c, False), start)
        top, total, accum = step(last, carry, True)
        wide = accum * (1.0 / total)
        wide_ref[:, cols] = wide
        lse_ref[:, cols] = top + jnp.log(total)
        pack_rows(wide, mixed_mine, tile)
        if number % 2:
            for target in range(4 * (number - 1), 4 * (number - 1) + 8):

                @pl.when(target != plane.me)
                def _(target=target):
                    mix.copy(target).start()

    mix.own().start()
    mix.take_all()
    unpack_into(mixed_ref, mixed_in)
    fold = Fold(team, part, near, far, fold_send, fold_recv)

    def branch(t):
        here = pl.ds(pl.multiple_of(t * 128, 128), 128)
        part[t] = matmul(mixed_ref[here, :], wo_ref[...]).astype(BF16)

    fold.send(branch)
    resid = x_ref[...].astype(F32) + fold.total() + params_ref[pl.ds(4, 1), :]
    resid_ref[...] = resid
    second[place.shard] = norm_parts(resid, params_ref[pl.ds(2, 1), :], params_ref[pl.ds(3, 1), :])[0].astype(BF16)
    share = Share(team, second, second.at[place.shard], share_send, share_recv)
    share.send()
    share.forward()
    dy.take()
    share.take()
    save_second = pltpu.make_async_copy(second, second_out, save_sem.at[3])
    save_second.start()
    for save in saves:
        save.wait()
    dy_own.wait()
    dy.sent()
    for item in heads:
        item.sent_all()

    def gone(j, c):
        for k in range(2):
            pass_on(k, j).wait_send()
        return c

    lax.fori_loop(0, 16, gone, 0)
    mix.sent_all()
    fold.sent()
    share.sent()
    save_second.wait()
    save_w.wait()
    vec.sent_all()
    columns.sent()
    x.sent()


def forward(*args):
    vmem = pl.BlockSpec(memory_space=pltpu.VMEM)
    anywhere = pl.BlockSpec(memory_space=pl.ANY)
    return pl.pallas_call(
        forward_kernel,
        name="forward",
        out_shape=[
            jax.ShapeDtypeStruct((512, 1024), BF16),
            jax.ShapeDtypeStruct((512, 256), BF16),
            jax.ShapeDtypeStruct((128, 1024), F32),
            jax.ShapeDtypeStruct((HALF, 2048), F32),
            jax.ShapeDtypeStruct((1, 2048), F32),
            jax.ShapeDtypeStruct((8, 1024), F32),
            jax.ShapeDtypeStruct((16, HALF, 128), BF16),
            jax.ShapeDtypeStruct((4096, 128), BF16),
            jax.ShapeDtypeStruct((4, 128, 1024), BF16),
            jax.ShapeDtypeStruct((4, 128, 1024), BF16),
            jax.ShapeDtypeStruct((3, 1024, 256), BF16),
        ],
        in_specs=[vmem] * 3 + [anywhere] * 4,
        out_specs=[vmem] * 6 + [anywhere] * 5,
        scratch_shapes=[
            pltpu.VMEM((4, 128, 1024), BF16),
            pltpu.VMEM((4, 8, 256), F32),
            pltpu.VMEM((3, 1024, 256), BF16),
            pltpu.VMEM((16, HALF, 128), BF16),
            pltpu.VMEM((4096, 128), BF16),
            pltpu.VMEM((16, HALF, 128), BF16),
            pltpu.VMEM((512, 512), BF16),
            pltpu.VMEM((2048, 128), BF16),
            pltpu.VMEM((128, 2048), BF16),
            pltpu.VMEM((128, 4096), BF16),
            pltpu.VMEM((16, HALF, 128), BF16),
            pltpu.VMEM((16, HALF, 128), BF16),
            pltpu.VMEM((4, 128, 1024), BF16),
            pltpu.VMEM((2, 128, 1024), BF16),
            pltpu.VMEM((128, 1024), BF16),
            pltpu.VMEM((4, 128, 1024), BF16),
            *swap_sems(5),
            *([pltpu.SemaphoreType.DMA((2, 16))] * 2),
            pltpu.SemaphoreType.DMA((5,)),
            *(TEAM_SEMS * 4),
            *COLUMN_SEMS,
        ],
        compiler_params=pltpu.CompilerParams(
            collective_id=1, has_side_effects=True, vmem_limit_bytes=VMEM_LIMIT
        ),
    )(*args)


def backward_kernel(
    second_ref, dy_ref, expand_ref, contract_ref, wo_ref, mixed_ref, resid_ref, bias_ref, params_ref,
    q_ref, kv_ref, wide_ref, lse_ref, first_in_ref, w_ref, x_ref,
    block_out, input_grad_ref, small_out, qkv_out, expand_out, contract_out, output_out,
    act, grad_pre, right, part, near, far, branch, sums_small,
    rows, turned, kv_turned, grad_rows, grad_turned, sums, packed, grad_mine, dq_mine, dkv_mine, dkv_in,
    big, stage, big_last, stage_last, dq_parts, dkv_parts,
    gq, gk, gv, qkv, qkv_stage, norm_send, norm_in, small_steps, small_in,
    swap_send, swap_recv, swap_local, big_local, big_send, big_recv, all_send, all_recv,
    half_send, half_recv, full_send, full_recv, small_send, small_recv, pair_send, pair_recv,
    *team_sems,
):
    place = Place()
    plane, pair, team = Plane(place), Pair(place), Team(place)
    column, cube = Column(place), Cube(place)
    half = query_half(place)
    sequence = place.spot // 4

    def swap(k, group, src, dst):
        return Swap(group, src, dst, swap_send.at[k], swap_recv.at[k], swap_local.at[k])

    def fold(k):
        return Fold(team, part.at[k], near.at[k], far.at[k], team_sems[2 * k], team_sems[2 * k + 1])

    meet([plane, pair, team, column])

    second_fold = fold(0)

    def make(t):
        pre = matmul(second_ref[t], expand_ref[...]) + bias_ref[...]
        value, slope = gelu_both(pre)
        act[t] = value.astype(BF16)
        grad = (matmul_nt(dy_ref[t], contract_ref[...]) * slope).astype(BF16)
        grad_pre[t] = grad
        part[0, t] = matmul_nt(grad, expand_ref[...]).astype(BF16)

    second_fold.send(make)

    def turn(src):
        for t in range(4):
            for at in range(0, src.shape[2], 256):
                right[pl.ds(at, 256), pl.ds(t * 128, 128)] = src[t, :, pl.ds(at, 256)].astype(F32).T.astype(BF16)

    def weight_grad(count, other, put):
        for at in range(0, count, 256):
            left = right[pl.ds(at, 256), :]
            total = matmul(left[:, :128], other[0])
            for t in range(1, 4):
                total = total + matmul(left[:, t * 128 : t * 128 + 128], other[t])
            put(at, total.astype(BF16))

    def bias_grad(row, src):
        total = jnp.sum(src[0].astype(F32), axis=0, keepdims=True)
        for t in range(1, 4):
            total = total + jnp.sum(src[t].astype(F32), axis=0, keepdims=True)
        sums_small[pl.ds(row, 1), :] = total

    halving = Halving(
        big_parts(cube),
        [big.at[k] for k in range(4)] + [big_last],
        [stage.at[k] for k in range(4)] + [stage_last],
        big_send, big_recv,
    )

    def put_contract(at, value):
        big[2 + at // 512, pl.ds(at % 512, 256), :] = value

    def put_expand(at, value):
        big[at // 512, pl.ds(at % 512, 256), :] = value

    def put_output(at, value):
        big_last[pl.ds(0, 256), :] = value[:, :512]
        big_last[pl.ds(256, 256), :] = value[:, 512:]

    turn(act)
    weight_grad(1024, dy_ref, put_contract)
    halving.send(0, (2, 3))
    bias_grad(1, dy_ref)
    bias_grad(2, grad_pre)
    grad_second = second_fold.total()
    gain = params_ref[pl.ds(2, 1), :]
    _, unit, inverse = norm_parts(resid_ref[...], gain, 0.0)
    grad_resid = dy_ref[place.shard].astype(F32) + norm_back(grad_second, unit, inverse, gain)
    sums_small[pl.ds(8, 1), :] = jnp.sum(grad_second * unit, axis=0, keepdims=True)
    sums_small[pl.ds(9, 1), :] = jnp.sum(grad_second, axis=0, keepdims=True)
    branch[place.shard] = grad_resid.astype(BF16)
    share = Share(team, branch, branch.at[place.shard], *team_sems[6:8])
    share.send()
    turn(second_ref)
    weight_grad(1024, grad_pre, put_expand)
    halving.send(0, (0, 1))
    share.forward()
    spread_rows(q_ref, rows, False, 0.125)
    turn_rows(rows, turned, 2048)
    turn_rows(kv_ref, kv_turned, 4096)
    for at in range(0, 4096, TILE):
        sums[pl.ds(at, TILE), :] = jnp.zeros((TILE, 128), F32)
    share.take()
    for t in range(4):
        grad_mixed = matmul_nt(branch[t], wo_ref[...]).astype(BF16)
        for two in range(2):
            lanes = slice(two * 128, two * 128 + 128)
            at = t * 4 + two * 2
            packed[at], packed[at + 1] = swap_heads(grad_mixed[:HALF, lanes], grad_mixed[HALF:, lanes])
    to_heads = swap(0, plane, lambda t: packed.at[t], lambda j, t: grad_mine.at[j])
    to_heads.send_all()
    for t in range(4):
        right[pl.ds(0, 256), pl.ds(t * 128, 128)] = mixed_ref[pl.ds(t * 128, 128), :].astype(F32).T.astype(BF16)
    weight_grad(256, branch, put_output)
    halving.send(0, (4,))
    ffn_fold = fold(1)

    def make_ffn(t):
        part[1, t] = matmul(act[t], contract_ref[...]).astype(BF16)

    ffn_fold.send(make_ffn)
    bias_grad(0, branch)

    dq = swap(1, plane, lambda t: dq_mine.at[t], lambda j, t: dq_parts.at[j])
    dkv = [
        swap(
            2 + k, plane,
            lambda t, k=k: dkv_mine.at[kv_place(half_of(place.layer) * 16 + t, k == 0)],
            lambda j, t, k=k: kv_block(dkv_parts, j, k == 0),
        )
        for k in range(2)
    ]

    def half_of(layer):
        return (layer + place.shard // 2 + sequence // 2) % 2

    def piece_rows(layer, k):
        start = half_of(layer) * 1024
        start = (3072 - start if k >= 2 else start) + (k % 2) * TILE
        return pl.ds(pl.multiple_of(start, TILE), TILE)

    def give(k):
        return pltpu.make_async_remote_copy(
            src_ref=dkv_mine.at[piece_rows(1 - place.layer, k)],
            dst_ref=dkv_in.at[k],
            send_sem=pair_send.at[k],
            recv_sem=pair_recv.at[k],
            device_id=pair.device(1 - place.layer),
            device_id_type=MESH,
        )

    to_heads.take_all()
    spread_rows(grad_mine, grad_rows, True, 1.0)
    turn_rows(grad_rows, grad_turned, 2048)
    for number, tile in enumerate((0, 3, 1, 2)):
        cols = pl.ds(tile * TILE, TILE)
        last = tile_place(half, tile)
        delta = jnp.sum(grad_turned[HALF:, cols].astype(F32) * wide_ref[:, cols], axis=0, keepdims=True)
        lse = lse_ref[:, cols]

        def step(kt, accum, masked):
            kv = kv_ref[key_rows(kt), :]
            scores = matmul(kv, turned[:, cols])
            if masked:
                scores = hide_later(scores)
            probs = jnp.exp(scores - lse)
            grad_probs = matmul(kv, grad_turned[:, cols])
            grad_scores = (probs * (grad_probs - delta)).astype(BF16)
            sums[key_rows(kt), :] += matmul(probs.astype(BF16), grad_rows[cols, :]) + matmul(
                grad_scores, rows[cols, :]
            )
            return accum + matmul(kv_turned[:HALF, key_rows(kt)], grad_scores)

        accum = lax.fori_loop(
            0, last, lambda kt, c: step(kt, c, False), jnp.zeros((HALF, TILE), F32)
        )
        accum = step(last, accum, True)
        pack_rows(accum * 0.125, dq_mine, tile)
        if number < 3:
            halving.add(number)
            halving.send(number + 1)
    for k in range(4):
        theirs = piece_rows(1 - place.layer, k)
        dkv_mine[theirs, :] = sums[theirs, :].astype(BF16)
        give(k).start()
    dq.send_all()
    halving.add(3)
    halving.send(4)
    for k in range(4):
        mine = piece_rows(place.layer, k)
        give(k).wait_recv()
        dkv_mine[mine, :] = (sums[mine, :] + dkv_in[k].astype(F32)).astype(BF16)
        for block in range(8):
            spot = (k % 2) * 8 + block if k < 2 else 15 - ((k % 2) * 8 + block)

            @pl.when(spot != plane.me)
            def _(spot=spot, k=k):
                dkv[k // 2].copy(spot).start()

    for item in dkv:
        item.own().start()
    halving.add(4)
    outs = [expand_out.at[0], expand_out.at[1], contract_out.at[0], contract_out.at[1], output_out]
    gather = Doubling(halving.parts, outs, all_send, all_recv)
    starts = [
        pltpu.make_async_copy(
            piece.view(halving.buffers[k], piece.held[5]), piece.view(outs[k], piece.held[5]), big_local.at[k]
        )
        for k, piece in enumerate(gather.parts)
    ]
    for start in starts:
        start.start()
    block_out[...] = (resid_ref[...] + ffn_fold.total() + params_ref[pl.ds(5, 1), :]).astype(BF16)
    for at in range(0, 1024, 256):
        right[pl.ds(at, 256), :] = first_in_ref[:, pl.ds(at, 256)].astype(F32).T.astype(BF16)
    for start in starts:
        start.wait()
    gather.send(3)

    parts = [Part(cube, 2 * k, 256, 16) for k in range(3)]
    qkv_halving = Halving(
        parts, [qkv.at[k] for k in range(3)], [qkv_stage.at[k] for k in range(3)], half_send, half_recv
    )

    def projection_grad(k, grad):
        for f in range(4):
            qkv[k, :, pl.ds(f * 256, 256)] = matmul(right[pl.ds(f * 256, 256), :], grad[...]).astype(BF16)
        qkv_halving.send(0, (k,))

    dq.take_all()
    unpack_into(gq, dq_parts)
    projection_grad(0, gq)
    for item in dkv:
        item.take_all()
    for at in range(0, 512, 128):
        here = pl.ds(at, 128)
        for two in range(2):
            lanes = pl.ds(two * 128, 128)
            gk[here, lanes], gv[here, lanes] = swap_heads(
                dkv_parts[here, two * 256 : two * 256 + 128], dkv_parts[here, two * 256 + 128 : two * 256 + 256]
            )
    projection_grad(1, gk)
    projection_grad(2, gv)
    first_fold = fold(2)

    def make_first(t):
        here = pl.ds(pl.multiple_of(t * 128, 128), 128)
        part[2, t] = (
            matmul_nt(gq[here, :], w_ref[0])
            + matmul_nt(gk[here, :], w_ref[1])
            + matmul_nt(gv[here, :], w_ref[2])
        ).astype(BF16)

    first_fold.send(make_first)
    for step in range(2):
        gather.take(3 - step)
        gather.send(2 - step)
        qkv_halving.add(step)
        qkv_halving.send(step + 1)
    grad_first = first_fold.total()
    gain = params_ref[pl.ds(0, 1), :]
    _, unit, inverse = norm_parts(x_ref[...].astype(F32), gain, 0.0)
    input_grad_ref[...] = (grad_resid + norm_back(grad_first, unit, inverse, gain)).astype(BF16)
    norm_rows = [
        jnp.sum(grad_first * unit, axis=0, keepdims=True),
        jnp.sum(grad_first, axis=0, keepdims=True),
    ]
    norm_send[...] = jnp.zeros_like(norm_send)
    for t in range(4):
        for k in range(2):
            norm_send[t, pl.ds(k, 1), :] = norm_rows[k][:, t * 256 : t * 256 + 256]
            norm_send[t, pl.ds(2 + k, 1), :] = sums_small[pl.ds(8 + k, 1), pl.ds(t * 256, 256)]
    to_column = swap(4, column, lambda t: norm_send.at[t], lambda j, t: norm_in.at[j])
    to_column.send_all()
    for step in range(2, 5):
        if step == 2:
            gather.take(1)
            gather.send(0)
        qkv_halving.add(step)
        if step < 4:
            qkv_halving.send(step + 1)
    cross = []
    for k, piece in enumerate(parts):
        row, _ = piece.held[5]

        def block(ref, f, row=row):
            return ref.at[
                pl.ds(pl.multiple_of(row, 16), 16), pl.ds(pl.multiple_of(f * 256, 256), 256)
            ]

        cross.append(swap(
            5 + k, column,
            lambda t, k=k, block=block: block(qkv.at[k], t),
            lambda j, t, k=k, block=block: block(qkv_out.at[k], j),
        ))
    for item in cross:
        item.send_all()
    to_column.take_all()
    small = small_steps.at[0]
    small[pl.ds(0, 8), :] = norm_in[0] + norm_in[1] + norm_in[2] + norm_in[3]
    small[pl.ds(4, 1), :] = jnp.sum(gq[...].astype(F32), axis=0, keepdims=True)
    small[pl.ds(5, 1), :] = jnp.sum(gv[...].astype(F32), axis=0, keepdims=True)
    own_lanes = pl.ds(pl.multiple_of(place.shard * 256, 256), 256)
    small[pl.ds(6, 1), :] = sums_small[pl.ds(0, 1), own_lanes]
    small[pl.ds(7, 1), :] = sums_small[pl.ds(1, 1), own_lanes]
    small[pl.ds(8, 8), :] = jnp.zeros((8, 256), F32)
    for t in range(4):
        small[pl.ds(8 + t, 1), :] = sums_small[pl.ds(2, 1), pl.ds(t * 256, 256)]
    full = Doubling(parts, [qkv_out.at[k] for k in range(3)], full_send, full_recv)

    def small_copy(step):
        return pltpu.make_async_remote_copy(
            src_ref=small_steps.at[step],
            dst_ref=small_in.at[step],
            send_sem=small_send.at[step],
            recv_sem=small_recv.at[step],
            device_id=cube.device(step),
            device_id_type=MESH,
        )

    small_copy(0).start()
    for item in cross:
        item.take_all()
    for step in range(5):
        if step > 0:
            full.send(4 - step)
            small_copy(step).start()
            full.take(4 - step)
        small_copy(step).wait_recv()
        small_steps[step + 1] = small_steps[step] + small_in[step]
    small_out[...] = small_steps[5]
    gather.take(0)
    for item in [to_heads, dq, *dkv, to_column, *cross]:
        item.sent_all()
    for item in (second_fold, ffn_fold, first_fold, share):
        item.sent()
    for item in (halving, gather, qkv_halving, full):
        item.finish()
    for k in range(4):
        give(k).wait_send()
    for step in range(5):
        small_copy(step).wait_send()


def backward(*args):
    vmem = pl.BlockSpec(memory_space=pltpu.VMEM)
    anywhere = pl.BlockSpec(memory_space=pl.ANY)
    blocks = pltpu.VMEM((4, 128, 1024), BF16)
    heads = pltpu.VMEM((16, HALF, 128), BF16)
    return pl.pallas_call(
        backward_kernel,
        name="backward",
        out_shape=[
            jax.ShapeDtypeStruct((128, 1024), BF16),
            jax.ShapeDtypeStruct((128, 1024), BF16),
            jax.ShapeDtypeStruct((16, 256), F32),
            jax.ShapeDtypeStruct((3, 256, 1024), BF16),
            jax.ShapeDtypeStruct((2, 512, 1024), BF16),
            jax.ShapeDtypeStruct((2, 512, 1024), BF16),
            jax.ShapeDtypeStruct((512, 512), BF16),
        ],
        in_specs=[vmem] * len(args),
        out_specs=[vmem] * 3 + [anywhere] * 4,
        scratch_shapes=[
            blocks,
            blocks,
            pltpu.VMEM((1024, 512), BF16),
            pltpu.VMEM((3, 4, 128, 1024), BF16),
            pltpu.VMEM((3, 2, 128, 1024), BF16),
            pltpu.VMEM((3, 128, 1024), BF16),
            blocks,
            pltpu.VMEM((16, 1024), F32),
            pltpu.VMEM((2048, 128), BF16),
            pltpu.VMEM((128, 2048), BF16),
            pltpu.VMEM((128, 4096), BF16),
            pltpu.VMEM((2048, 128), BF16),
            pltpu.VMEM((128, 2048), BF16),
            pltpu.VMEM((4096, 128), F32),
            heads,
            heads,
            heads,
            pltpu.VMEM((4096, 128), BF16),
            pltpu.VMEM((4, TILE, 128), BF16),
            pltpu.VMEM((4, 512, 1024), BF16),
            pltpu.VMEM((4, 512, 1024), BF16),
            pltpu.VMEM((512, 512), BF16),
            pltpu.VMEM((512, 512), BF16),
            heads,
            pltpu.VMEM((512, 512), BF16),
            pltpu.VMEM((512, 256), BF16),
            pltpu.VMEM((512, 256), BF16),
            pltpu.VMEM((512, 256), BF16),
            pltpu.VMEM((3, 256, 1024), BF16),
            pltpu.VMEM((3, 256, 1024), BF16),
            pltpu.VMEM((4, 8, 256), F32),
            pltpu.VMEM((4, 8, 256), F32),
            pltpu.VMEM((6, 16, 256), F32),
            pltpu.VMEM((5, 16, 256), F32),
            *swap_sems(8),
            pltpu.SemaphoreType.DMA((5,)),
            *([pltpu.SemaphoreType.DMA((5, 5))] * 4),
            *([pltpu.SemaphoreType.DMA((3, 5))] * 4),
            *([pltpu.SemaphoreType.DMA((5,))] * 2),
            *([pltpu.SemaphoreType.DMA((4,))] * 2),
            *(TEAM_SEMS * 4),
        ],
        compiler_params=pltpu.CompilerParams(
            collective_id=2, has_side_effects=True, vmem_limit_bytes=VMEM_LIMIT
        ),
    )(*args)


def on_device(
    tokens, query_weight, key_weight, value_weight, output_weight, expand_weight, contract_weight,
    query_bias, value_bias, output_bias, expand_bias, contract_bias,
    first_gain, first_shift, second_gain, second_shift, cotangent,
):
    vectors = [
        first_gain, first_shift, second_gain, second_shift, output_bias, contract_bias, query_bias, value_bias
    ]
    vectors = jnp.concatenate(vectors).astype(F32).reshape(8, 256)
    first_in, mixed, resid, wide, lse, params, q_mine, kv_mine, dy_all, second_in, weights = forward(
        tokens[0], vectors, output_weight, cotangent[0], query_weight, key_weight, value_weight
    )
    block_output, input_grad, small, qkv, expand, contract, output = backward(
        second_in, dy_all, expand_weight, contract_weight, output_weight, mixed, resid,
        expand_bias[None].astype(F32), params,
        q_mine, kv_mine, wide, lse, first_in, weights, tokens[0],
    )
    return (
        block_output[None],
        input_grad[None],
        qkv[0].astype(F32),
        qkv[1].astype(F32),
        qkv[2].astype(F32),
        jnp.concatenate([output[:256], output[256:]], axis=1).astype(F32),
        expand.reshape(1024, 1024).astype(F32),
        contract.reshape(1024, 1024).astype(F32),
        small[4],
        small[5],
        small[6],
        small[8:12].reshape(1024),
        small[7],
        small[0],
        small[1],
        small[2],
        small[3],
    )


def solution(mesh):
    weights = [P("fsdp", None)] * 4 + [P(None, "fsdp"), P("fsdp", None)]
    rows = P("fsdp", "seq", None)
    return jax.shard_map(
        on_device,
        mesh=mesh,
        in_specs=(rows, *weights, *([P("fsdp")] * 9), rows),
        out_specs=(rows, rows, *weights, *([P("fsdp")] * 9)),
        check_vma=False,
    )
```

```python
import functools

import jax
import jax.numpy as jnp
from jax import lax
from jax.experimental import pallas as pl
from jax.experimental.pallas import tpu as pltpu
from jax.sharding import PartitionSpec as P

MESH = pl.DeviceIdType.MESH
BF16 = jnp.bfloat16
F32 = jnp.float32
TILE = 512
HALF = 64
VMEM_LIMIT = 60 * 1024 * 1024


def matmul(left, right):
    return jnp.dot(left, right, preferred_element_type=F32)


def matmul_tn(left, right):
    return lax.dot_general(left, right, (((0,), (0,)), ((), ())), preferred_element_type=F32)


def matmul_nt(left, right):
    return lax.dot_general(left, right, (((1,), (1,)), ((), ())), preferred_element_type=F32)


def norm_parts(values, gain, shift):
    mean = jnp.mean(values, axis=-1, keepdims=True)
    centered = values - mean
    variance = jnp.mean(centered * centered, axis=-1, keepdims=True)
    inverse = lax.rsqrt(variance + 1e-05)
    normed = centered * inverse
    return (normed * gain + shift, normed, inverse)


def norm_back(grad, normed, inverse, gain):
    scaled = grad * gain
    return inverse * (
        scaled
        - jnp.mean(scaled, axis=-1, keepdims=True)
        - normed * jnp.mean(scaled * normed, axis=-1, keepdims=True)
    )


def gelu_both(values):
    square = values * values
    inner = jnp.tanh(0.7978845608028654 * (values + 0.044715 * square * values))
    value = 0.5 * values * (1.0 + inner)
    slope = 0.5 * (1.0 + inner) + 0.5 * values * (1.0 - inner * inner) * 0.7978845608028654 * (
        1.0 + 0.134145 * square
    )
    return value, slope


class Place:
    def __init__(self):
        self.seq = lax.axis_index("seq")
        self.shard = lax.axis_index("fsdp")
        self.layer = self.seq // 16
        self.spot = self.seq % 16
        self.team = (self.layer + self.shard // 2) % 2


class Team:
    size = 4

    def __init__(self, place):
        self.place = place
        self.me = place.shard

    def device(self, t):
        return {"seq": ((self.place.team + t // 2) % 2) * 16 + self.place.spot, "fsdp": t}


class Plane:
    size = 16

    def __init__(self, place):
        self.place = place
        self.me = place.spot

    def device(self, t):
        return {"seq": self.place.layer * 16 + t, "fsdp": self.place.shard}


class Line:
    size = 32

    def __init__(self, place):
        self.place = place
        self.me = place.seq

    def device(self, t):
        return {"seq": t, "fsdp": self.place.shard}


def spread(count, body):
    if count <= 4:
        for step in range(count):
            body(step)
    else:
        lax.fori_loop(0, count, lambda step, c: (body(step), c)[1], 0)


def query_half(place):
    return (place.layer + place.shard // 2 + place.spot // 8) % 2


def tile_place(half, tile):
    return half * 2 + tile if tile < 2 else 6 - 2 * half + tile - 2


def spread_rows(src_ref, out_ref, at_high, factor):
    lane = lax.broadcasted_iota(jnp.int32, (HALF, 128), 1)
    keep = (lane >= HALF) if at_high else (lane < HALF)
    for block in range(16):
        both = src_ref[block].astype(F32) * factor
        moved = pltpu.roll(both, HALF, 1)
        low, high = (moved, both) if at_high else (both, moved)
        out_ref[pl.ds(block * HALF, HALF), :] = jnp.where(keep, low, 0.0).astype(BF16)
        out_ref[pl.ds(1024 + (15 - block) * HALF, HALF), :] = jnp.where(keep, high, 0.0).astype(BF16)


def turn_rows(src_ref, out_ref, rows):
    for at in range(0, rows, TILE):
        out_ref[:, pl.ds(at, TILE)] = src_ref[pl.ds(at, TILE), :].astype(F32).T.astype(BF16)


def pack_rows(turned, out_ref, tile):
    empty = jnp.zeros_like(turned)
    if tile < 2:
        rows = jnp.concatenate([turned, empty], axis=0).T.astype(BF16)
        for part in range(8):
            out_ref[tile * 8 + part] = rows[part * HALF : (part + 1) * HALF]
    else:
        rows = jnp.concatenate([empty, turned], axis=0).T.astype(BF16)
        for part in range(8):
            block = 15 - ((tile - 2) * 8 + part)
            out_ref[block] = out_ref[block] + rows[part * HALF : (part + 1) * HALF]


def key_rows(kt):
    return pl.ds(pl.multiple_of(kt * TILE, TILE), TILE)


def other_tiles(half, tile):
    if tile < 2:
        return 2 - 2 * half, 2
    return 2 - 2 * half, 6 - 4 * half


def hide_later(scores):
    key = lax.broadcasted_iota(jnp.int32, (TILE, TILE), 0)
    query = lax.broadcasted_iota(jnp.int32, (TILE, TILE), 1)
    return jnp.where(key <= query, scores, -1e30)


def stored_block(sender_team, spot, sequence):
    return ((sender_team + sequence // 2) % 2) * 16 + spot


def swap_heads(low, high):
    low, high = low.astype(F32), high.astype(F32)
    left = lax.broadcasted_iota(jnp.int32, low.shape, 1) < HALF
    one = jnp.where(left, low, pltpu.roll(high, HALF, 1))
    two = jnp.where(left, pltpu.roll(low, HALF, 1), high)
    return one.astype(BF16), two.astype(BF16)


def head_pieces(sequence, pair):
    low = pl.ds(sequence * 128, HALF)
    high = pl.ds(sequence * 128 + HALF, HALF)
    lanes = pl.ds(pair * 128, 128)
    return (low, lanes), (high, lanes), sequence * 4 + pair * 2


def pack_into(out_ref, src_ref):
    for sequence in range(4):
        for pair in range(2):
            low, high, at = head_pieces(sequence, pair)
            out_ref[at], out_ref[at + 1] = swap_heads(src_ref[low], src_ref[high])


def unpack_into(out_ref, src_ref):
    for sequence in range(4):
        for pair in range(2):
            low, high, at = head_pieces(sequence, pair)
            out_ref[low], out_ref[high] = swap_heads(src_ref[at], src_ref[at + 1])


def kv_block(ref, spot, low):
    rows = pl.ds(pl.multiple_of((spot // 4) * 128 + (0 if low else HALF), HALF), HALF)
    return ref.at[rows, pl.ds(pl.multiple_of((spot % 4) * 128, 128), 128)]


def kv_place(block, low):
    return pl.ds(pl.multiple_of((block if low else 63 - block) * HALF, HALF), HALF)


class Column:
    size = 4

    def __init__(self, place):
        self.place = place
        self.me = place.shard

    def device(self, t):
        return {"seq": self.place.seq, "fsdp": t}


class Cube:
    def __init__(self, place):
        x, z = place.spot // 4, place.spot % 4
        self.shard = place.shard
        self.bits = [(x + x // 2) % 2, x // 2, (z + z // 2) % 2, z // 2, place.layer]

        def at(x, z, layer):
            return layer * 16 + x * 4 + z

        self.partners = [
            at(x + 1 - 2 * (x % 2), z, place.layer),
            at(3 - x, z, place.layer),
            at(x, z + 1 - 2 * (z % 2), place.layer),
            at(x, 3 - z, place.layer),
            at(x, z, 1 - place.layer),
        ]

    def device(self, bit):
        return {"seq": self.partners[bit], "fsdp": self.shard}


class Part:
    def __init__(self, cube, index, rows, least):
        self.cube = cube
        self.order = [(index + s) % 5 for s in range(5)]
        row = 0
        self.sent, self.held, self.halves = [], [(0, rows)], []
        for bit in self.order:
            value = cube.bits[bit]
            self.halves.append(rows > least)
            if rows > least:
                rows //= 2
                self.sent.append((row + (1 - value) * rows, rows))
                row = row + value * rows
            else:
                self.sent.append((row, rows))
            self.held.append((row, rows))

    def view(self, ref, region):
        row, rows = region
        return ref.at[pl.ds(row if isinstance(row, int) else pl.multiple_of(row, 16), rows)]

    def stage(self, step):
        rows = self.sent[step][1]
        return (rows if self.halves[step] else 0, rows)


class Halving:
    def __init__(self, parts, buffers, stages, send_sem, recv_sem):
        self.parts, self.buffers, self.stages = parts, buffers, stages
        self.send_sem, self.recv_sem = send_sem, recv_sem

    def copy(self, k, step):
        part = self.parts[k]
        return pltpu.make_async_remote_copy(
            src_ref=part.view(self.buffers[k], part.sent[step]),
            dst_ref=part.view(self.stages[k], part.stage(step)),
            send_sem=self.send_sem.at[k, step],
            recv_sem=self.recv_sem.at[k, step],
            device_id=part.cube.device(part.order[step]),
            device_id_type=MESH,
        )

    def send(self, step, which=None):
        for k in which or range(len(self.parts)):
            self.copy(k, step).start()

    def add(self, step):
        for k, part in enumerate(self.parts):
            self.copy(k, step).wait_recv()
            if not part.halves[step]:
                self.copy(k, step).wait_send()
            mine = part.view(self.buffers[k], part.held[step + 1])
            other = part.view(self.stages[k], part.stage(step))
            rows = part.held[step + 1][1]

            def slab(at, c, mine=mine, other=other):
                here = pl.ds(pl.multiple_of(at * 16, 16), 16)
                mine[here, :] = (mine[here, :].astype(F32) + other[here, :].astype(F32)).astype(BF16)
                return c

            if rows == 16:
                slab(0, 0)
            else:
                lax.fori_loop(0, rows // 16, slab, 0)

    def finish(self):
        for k, part in enumerate(self.parts):
            for step in range(5):
                if part.halves[step]:
                    self.copy(k, step).wait_send()


class Doubling:
    def __init__(self, parts, buffers, send_sem, recv_sem):
        self.parts, self.buffers = parts, buffers
        self.send_sem, self.recv_sem = send_sem, recv_sem

    def copy(self, k, step):
        part = self.parts[k]
        view = part.view(self.buffers[k], part.held[step + 1])
        return pltpu.make_async_remote_copy(
            src_ref=view,
            dst_ref=view,
            send_sem=self.send_sem.at[k, step],
            recv_sem=self.recv_sem.at[k, step],
            device_id=part.cube.device(part.order[step]),
            device_id_type=MESH,
        )

    def landed(self, k, step):
        part = self.parts[k]
        view = part.view(self.buffers[k], part.sent[step])
        return pltpu.make_async_remote_copy(
            src_ref=view,
            dst_ref=view,
            send_sem=self.send_sem.at[k, step],
            recv_sem=self.recv_sem.at[k, step],
            device_id=part.cube.device(part.order[step]),
            device_id_type=MESH,
        )

    def send(self, step):
        for k in range(len(self.parts)):
            self.copy(k, step).start()

    def take(self, step):
        for k in range(len(self.parts)):
            self.landed(k, step).wait_recv()

    def finish(self):
        for k in range(len(self.parts)):
            for step in range(4):
                self.copy(k, step).wait_send()


def big_parts(cube):
    return [Part(cube, k, 512, 32) for k in range(5)]


def meet(groups):
    barrier = pltpu.get_barrier_semaphore()
    for grp in groups:

        def hello(step, grp=grp):
            pl.semaphore_signal(
                barrier, inc=1, device_id=grp.device((grp.me + 1 + step) % grp.size), device_id_type=MESH
            )

        spread(grp.size - 1, hello)
    pl.semaphore_wait(barrier, sum(grp.size - 1 for grp in groups))


class Swap:
    def __init__(self, group, src, dst, send_sem, recv_sem, local_sem):
        self.group, self.src, self.dst = group, src, dst
        self.send_sem, self.recv_sem, self.local_sem = send_sem, recv_sem, local_sem

    def copy(self, target):
        return pltpu.make_async_remote_copy(
            src_ref=self.src(target),
            dst_ref=self.dst(self.group.me, target),
            send_sem=self.send_sem.at[target],
            recv_sem=self.recv_sem.at[self.group.me],
            device_id=self.group.device(target),
            device_id_type=MESH,
        )

    def landed(self, sender):
        view = self.dst(sender, self.group.me)
        return pltpu.make_async_remote_copy(
            src_ref=view,
            dst_ref=view,
            send_sem=self.send_sem.at[sender],
            recv_sem=self.recv_sem.at[sender],
            device_id=self.group.device(sender),
            device_id_type=MESH,
        )

    def own(self):
        return pltpu.make_async_copy(
            self.src(self.group.me), self.dst(self.group.me, self.group.me), self.local_sem
        )

    def send(self, step):
        self.copy((self.group.me + 1 + step) % self.group.size).start()

    def take(self, step):
        self.landed((self.group.me + 1 + step) % self.group.size).wait_recv()

    def sent(self, step):
        self.copy((self.group.me + 1 + step) % self.group.size).wait_send()

    def send_all(self):
        spread(self.group.size - 1, self.send)
        self.own().start()

    def take_all(self):
        spread(self.group.size - 1, self.take)
        self.own().wait()

    def sent_all(self):
        spread(self.group.size - 1, self.sent)


def swap_sems(count):
    return [
        pltpu.SemaphoreType.DMA((count, 32)),
        pltpu.SemaphoreType.DMA((count, 32)),
        pltpu.SemaphoreType.DMA((count,)),
    ]


class Square:
    size = 4

    def __init__(self, place):
        self.place = place
        self.x, self.z = place.spot // 4, place.spot % 4
        self.me = ((self.x + self.x // 2) % 2) * 2 + (self.z + self.z // 2) % 2

    def device(self, t):
        x = 2 * (self.x // 2) + (t // 2 + self.x // 2) % 2
        z = 2 * (self.z // 2) + (t % 2 + self.z // 2) % 2
        return {"seq": self.place.layer * 16 + x * 4 + z, "fsdp": self.place.shard}


class Columns:
    def __init__(self, team, square, sources, out, sems):
        self.team, self.square, self.sources, self.out = team, square, sources, out
        self.near_send, self.near_recv, self.far_send, self.far_recv, self.pass_send, self.pass_recv, self.local = sems
        me = team.me
        self.me = me
        self.sibling = (me // 2) * 2 + 1 - me % 2
        across = (me + 2) % 4
        self.far = (across, (self.sibling + 2) % 4)

    def lanes(self, member):
        return pl.ds(pl.multiple_of(member * 256, 256), 256)

    def block(self, k, member):
        return self.out.at[k, self.lanes(member)]

    def quarter(self, k, member, spot):
        return self.out.at[k, pl.ds(pl.multiple_of(member * 256 + spot * 64, 64), 64)]

    def remote(self, src, dst, send_sem, recv_sem, device):
        return pltpu.make_async_remote_copy(
            src_ref=src, dst_ref=dst, send_sem=send_sem, recv_sem=recv_sem, device_id=device, device_id_type=MESH
        )

    def near(self, k, arriving=False):
        dst = self.block(k, self.sibling if arriving else self.me)
        src = dst if arriving else self.sources[k].at[:, self.lanes(self.sibling)]
        return self.remote(src, dst, self.near_send.at[k], self.near_recv.at[k], self.team.device(self.sibling))

    def far_copy(self, k, which, arriving=False):
        other = self.far[which]
        dst = self.quarter(k, other if arriving else self.me, self.square.me)
        rows = pl.ds(pl.multiple_of(self.square.me * 64, 64), 64)
        src = dst if arriving else self.sources[k].at[rows, self.lanes(other)]
        at = which * 3 + k
        return self.remote(src, dst, self.far_send.at[at], self.far_recv.at[at], self.team.device(other))

    def pass_copy(self, k, which, step, arriving=False):
        spot = (self.square.me + 1 + step) % 4
        view = self.quarter(k, self.far[which], spot if arriving else self.square.me)
        at = which * 3 + k
        return self.remote(
            view, view, self.pass_send.at[at, spot], self.pass_recv.at[at, spot if arriving else self.square.me],
            self.square.device(spot),
        )

    def own(self, k):
        return pltpu.make_async_copy(self.sources[k].at[:, self.lanes(self.me)], self.block(k, self.me), self.local.at[k])

    def send(self):
        for k in range(3):
            for which in range(2):
                self.far_copy(k, which).start()
        for k in range(3):
            self.near(k).start()
            self.own(k).start()

    def forward(self):
        for k in range(3):
            for which in range(2):
                self.far_copy(k, which, True).wait_recv()
                for step in range(3):
                    self.pass_copy(k, which, step).start()

    def take(self):
        for k in range(3):
            self.own(k).wait()
            self.near(k, True).wait_recv()
            for which in range(2):
                for step in range(3):
                    self.pass_copy(k, which, step, True).wait_recv()

    def sent(self):
        for k in range(3):
            self.near(k).wait_send()
            for which in range(2):
                self.far_copy(k, which).wait_send()
                for step in range(3):
                    self.pass_copy(k, which, step).wait_send()


COLUMN_SEMS = [
    *([pltpu.SemaphoreType.DMA((3,))] * 2),
    *([pltpu.SemaphoreType.DMA((6,))] * 2),
    *([pltpu.SemaphoreType.DMA((6, 4))] * 2),
    pltpu.SemaphoreType.DMA((3,)),
]


class Pair:
    size = 2

    def __init__(self, place):
        self.place = place
        self.me = place.layer

    def device(self, t):
        return {"seq": t * 16 + self.place.spot, "fsdp": self.place.shard}


class Fold:
    def __init__(self, team, part, near, far, send_sem, recv_sem):
        self.team, self.part, self.near, self.far = team, part, near, far
        self.send_sem, self.recv_sem = send_sem, recv_sem
        me = team.me
        self.me = me
        self.sibling = (me // 2) * 2 + 1 - me % 2
        self.across = (me + 2) % 4
        self.opposite = (self.sibling + 2) % 4

    def copy(self, k):
        if k < 2:
            src, dst, to = self.part.at[(self.opposite, self.sibling)[k]], self.near.at[k], self.sibling
        else:
            src, dst, to = self.part.at[self.across], self.far, self.across
        return pltpu.make_async_remote_copy(
            src_ref=src,
            dst_ref=dst,
            send_sem=self.send_sem.at[k],
            recv_sem=self.recv_sem.at[k],
            device_id=self.team.device(to),
            device_id_type=MESH,
        )

    def send(self, make):
        make(self.opposite)
        self.copy(0).start()
        make(self.across)
        self.copy(0).wait_recv()
        self.part[self.across] = (
            self.part[self.across].astype(F32) + self.near[0].astype(F32)
        ).astype(BF16)
        self.copy(2).start()
        make(self.sibling)
        self.copy(1).start()
        make(self.me)

    def total(self):
        self.copy(1).wait_recv()
        self.copy(2).wait_recv()
        return self.part[self.me].astype(F32) + self.near[1].astype(F32) + self.far[...].astype(F32)

    def sent(self):
        for k in range(3):
            self.copy(k).wait_send()


class Share:
    def __init__(self, team, out, own, send_sem, recv_sem):
        self.team, self.out, self.own = team, out, own
        self.send_sem, self.recv_sem = send_sem, recv_sem
        me = team.me
        self.me = me
        self.sibling = (me // 2) * 2 + 1 - me % 2
        self.across = (me + 2) % 4
        self.opposite = (self.sibling + 2) % 4

    def rows(self, k):
        return pl.ds((k % 2) * 64, 64)

    def copy(self, k):
        kind = k // 2
        src = self.own.at[self.rows(k)] if kind < 2 else self.out.at[self.across, self.rows(k)]
        block = self.me if kind < 2 else self.across
        return pltpu.make_async_remote_copy(
            src_ref=src,
            dst_ref=self.out.at[block, self.rows(k)],
            send_sem=self.send_sem.at[k],
            recv_sem=self.recv_sem.at[k],
            device_id=self.team.device(self.across if kind == 1 else self.sibling),
            device_id_type=MESH,
        )

    def landed(self, k):
        view = self.out.at[(self.sibling, self.across, self.opposite)[k // 2], self.rows(k)]
        return pltpu.make_async_remote_copy(
            src_ref=view,
            dst_ref=view,
            send_sem=self.send_sem.at[k],
            recv_sem=self.recv_sem.at[k],
            device_id=self.team.device(self.across if k // 2 == 1 else self.sibling),
            device_id_type=MESH,
        )

    def send(self):
        for k in (2, 3, 0, 1):
            self.copy(k).start()

    def forward(self):
        for k in (2, 3):
            self.landed(k).wait_recv()
            self.copy(k + 2).start()

    def take(self):
        for k in (0, 1, 4, 5):
            self.landed(k).wait_recv()

    def sent(self):
        for k in range(6):
            self.copy(k).wait_send()


TEAM_SEMS = [pltpu.SemaphoreType.DMA((6,)), pltpu.SemaphoreType.DMA((6,))]


def forward_kernel(
    vec_ref, x_ref, wo_from, dy_ref, wq_ref, wk_ref, wv_ref,
    first_in_ref, mixed_ref, resid_ref, wide_ref, lse_ref, params_ref, q_out, kv_out, dy_out, second_out, w_out,
    x_all, vec_all, weights, totals, wo_ref,
    q_mine, kv_mine, q_send, kv_send, rows, turned, kv_turned, mixed_mine, mixed_in, part, near, far, second,
    swap_send, swap_recv, swap_local, pass_send, pass_recv, save_sem,
    dy_send, dy_recv, fold_send, fold_recv, share_send, share_recv, x_send, x_recv, *column_sems,
):
    place = Place()
    plane, pair, team = Plane(place), Pair(place), Team(place)
    half = query_half(place)
    sequence = place.spot // 4

    def swap(k, group, src, dst):
        return Swap(group, src, dst, swap_send.at[k], swap_recv.at[k], swap_local.at[k])

    meet([plane, pair, team])
    dy = Share(team, dy_out, dy_ref, dy_send, dy_recv)
    dy_own = pltpu.make_async_copy(dy_ref, dy_out.at[team.me], save_sem.at[0])
    vec = swap(4, team, lambda t: vec_ref, lambda j, t: vec_all.at[j])
    columns = Columns(team, Square(place), (wq_ref, wk_ref, wv_ref), weights, column_sems)
    x = Share(team, x_all, x_ref, x_send, x_recv)
    vec.send_all()
    columns.send()
    x.send()
    dy_own.start()
    x_own = pltpu.make_async_copy(x_ref, x_all.at[team.me], save_sem.at[5])
    load_wo = pltpu.make_async_copy(wo_from, wo_ref, save_sem.at[6])
    x_own.start()
    load_wo.start()
    columns.forward()
    x.forward()
    dy.send()
    vec.take_all()
    for t in range(4):
        params_ref[:, pl.ds(t * 256, 256)] = vec_all[t]
    x.take()
    x_own.wait()
    columns.take()
    save_w = pltpu.make_async_copy(weights, w_out, save_sem.at[4])
    save_w.start()

    def kv_rows(layer, spot, seq, low):
        return kv_place(stored_block((layer + place.shard // 2) % 2, spot, seq), low)

    heads = [
        swap(
            k, plane,
            lambda t, k=k: kv_block(kv_send, t, k == 0),
            lambda j, t, k=k: kv_mine.at[kv_rows(place.layer, j, t // 4, k == 0)],
        )
        for k in range(2)
    ]
    heads.append(swap(2, plane, lambda t: q_send.at[t], lambda j, t: q_mine.at[j]))
    gain, shift = params_ref[pl.ds(0, 1), :], params_ref[pl.ds(1, 1), :]
    for turn in range(4):
        s = (sequence + 1 + turn) % 4
        normed = norm_parts(x_all[s].astype(F32), gain, shift)[0].astype(BF16)
        first_in_ref[pl.ds(pl.multiple_of(s * 128, 128), 128), :] = normed
        query = (matmul(normed, weights[0]) + vec_ref[pl.ds(6, 1), :]).astype(BF16)
        key = matmul(normed, weights[1]).astype(BF16)
        value = (matmul(normed, weights[2]) + vec_ref[pl.ds(7, 1), :]).astype(BF16)
        for two in range(2):
            lanes = slice(two * 128, two * 128 + 128)
            at = s * 4 + two * 2
            for part_of in range(2):
                cut = slice(part_of * HALF, part_of * HALF + HALF)
                one, other = swap_heads(key[cut, lanes], value[cut, lanes])
                down = pl.ds(pl.multiple_of(s * 128 + part_of * HALF, HALF), HALF)
                kv_send[down, two * 256 : two * 256 + 128] = one
                kv_send[down, two * 256 + 128 : two * 256 + 256] = other
            q_send[at], q_send[at + 1] = swap_heads(query[:HALF, lanes], query[HALF:, lanes])
        for head in range(4 if turn < 3 else 3):
            target = s * 4 + (place.spot + 1 + head) % 4
            for item in heads:
                item.copy(target).start()

    for item in heads:
        item.own().start()

    def pass_on(k, j):
        view = kv_mine.at[kv_rows(place.layer, j, sequence, k == 0)]
        return pltpu.make_async_remote_copy(
            src_ref=view,
            dst_ref=view,
            send_sem=pass_send.at[k, j],
            recv_sem=pass_recv.at[k, j],
            device_id=pair.device(1 - place.layer),
            device_id_type=MESH,
        )

    def passed(k, j):
        view = kv_mine.at[kv_rows(1 - place.layer, j, sequence, k == 0)]
        return pltpu.make_async_remote_copy(
            src_ref=view,
            dst_ref=view,
            send_sem=pass_send.at[k, j],
            recv_sem=pass_recv.at[k, j],
            device_id=pair.device(1 - place.layer),
            device_id_type=MESH,
        )

    for item in heads:
        item.own().wait()
    for k in range(2):
        pass_on(k, plane.me).start()

    def relay(step, c):
        j = (plane.me + 15 - step) % 16
        for k in range(2):
            heads[k].landed(j).wait_recv()
            pass_on(k, j).start()
        heads[2].landed(j).wait_recv()
        return c

    lax.fori_loop(0, 15, relay, 0)
    spread_rows(q_mine, rows, False, 0.125)
    turn_rows(rows, turned, 2048)

    def turn_keys(kt):
        kv_turned[:, key_rows(kt)] = kv_mine[key_rows(kt), :].astype(F32).T.astype(BF16)

    def step(kt, carry, cols, masked):
        top, total, accum = carry
        scores = matmul(kv_mine[key_rows(kt), :], turned[:, cols])
        if masked:
            scores = hide_later(scores)
        new_top = jnp.maximum(top, jnp.max(scores, axis=0, keepdims=True))
        probs = jnp.exp(scores - new_top)
        fade = jnp.exp(top - new_top)
        total = total * fade + jnp.sum(probs, axis=0, keepdims=True)
        accum = accum * fade + matmul(kv_turned[HALF:, key_rows(kt)], probs.astype(BF16))
        return new_top, total, accum

    for tile in range(4):
        turn_keys(tile_place(half, tile))
    for tile in range(4):
        cols = pl.ds(tile * TILE, TILE)
        carry = (
            jnp.full((1, TILE), -1e30, F32),
            jnp.zeros((1, TILE), F32),
            jnp.zeros((HALF, TILE), F32),
        )
        for before in range(tile + 1):
            carry = step(tile_place(half, before), carry, cols, before == tile)
        lse_ref[:, cols], totals[:, cols], wide_ref[:, cols] = carry

    def arrive(j, c):
        for k in range(2):
            passed(k, j).wait_recv()
        return c

    lax.fori_loop(0, 16, arrive, 0)
    saves = [
        pltpu.make_async_copy(q_mine, q_out, save_sem.at[1]),
        pltpu.make_async_copy(kv_mine, kv_out, save_sem.at[2]),
    ]
    for save in saves:
        save.start()
    dy.forward()
    for tile in range(4):
        turn_keys(tile_place(1 - half, tile))
    mix = swap(3, plane, lambda t: mixed_mine.at[t], lambda j, t: mixed_in.at[j])
    for number, tile in enumerate((0, 3, 1, 2)):
        cols = pl.ds(tile * TILE, TILE)
        low, high = other_tiles(half, tile)
        top, total, accum = lax.fori_loop(
            low, high, lambda kt, c: step(kt, c, cols, False), (lse_ref[:, cols], totals[:, cols], wide_ref[:, cols])
        )
        wide = accum * (1.0 / total)
        wide_ref[:, cols] = wide
        lse_ref[:, cols] = top + jnp.log(total)
        pack_rows(wide, mixed_mine, tile)
        if number % 2:
            for target in range(4 * (number - 1), 4 * (number - 1) + 8):

                @pl.when(target != plane.me)
                def _(target=target):
                    mix.copy(target).start()

    mix.own().start()
    mix.take_all()
    unpack_into(mixed_ref, mixed_in)
    fold = Fold(team, part, near, far, fold_send, fold_recv)
    load_wo.wait()

    def branch(t):
        here = pl.ds(pl.multiple_of(t * 128, 128), 128)
        part[t] = matmul(mixed_ref[here, :], wo_ref[...]).astype(BF16)

    fold.send(branch)
    resid = x_all[place.shard].astype(F32) + fold.total() + params_ref[pl.ds(4, 1), :]
    resid_ref[...] = resid
    second[place.shard] = norm_parts(resid, params_ref[pl.ds(2, 1), :], params_ref[pl.ds(3, 1), :])[0].astype(BF16)
    share = Share(team, second, second.at[place.shard], share_send, share_recv)
    share.send()
    share.forward()
    dy.take()
    share.take()
    save_second = pltpu.make_async_copy(second, second_out, save_sem.at[3])
    save_second.start()
    for save in saves:
        save.wait()
    dy_own.wait()
    dy.sent()
    for item in heads:
        item.sent_all()

    def gone(j, c):
        for k in range(2):
            pass_on(k, j).wait_send()
        return c

    lax.fori_loop(0, 16, gone, 0)
    mix.sent_all()
    fold.sent()
    share.sent()
    save_second.wait()
    save_w.wait()
    vec.sent_all()
    columns.sent()
    x.sent()


def forward(*args):
    vmem = pl.BlockSpec(memory_space=pltpu.VMEM)
    anywhere = pl.BlockSpec(memory_space=pl.ANY)
    return pl.pallas_call(
        forward_kernel,
        name="forward",
        out_shape=[
            jax.ShapeDtypeStruct((512, 1024), BF16),
            jax.ShapeDtypeStruct((512, 256), BF16),
            jax.ShapeDtypeStruct((128, 1024), F32),
            jax.ShapeDtypeStruct((HALF, 2048), F32),
            jax.ShapeDtypeStruct((1, 2048), F32),
            jax.ShapeDtypeStruct((8, 1024), F32),
            jax.ShapeDtypeStruct((16, HALF, 128), BF16),
            jax.ShapeDtypeStruct((4096, 128), BF16),
            jax.ShapeDtypeStruct((4, 128, 1024), BF16),
            jax.ShapeDtypeStruct((4, 128, 1024), BF16),
            jax.ShapeDtypeStruct((3, 1024, 256), BF16),
        ],
        in_specs=[vmem] + [anywhere] * 6,
        out_specs=[vmem] * 6 + [anywhere] * 5,
        scratch_shapes=[
            pltpu.VMEM((4, 128, 1024), BF16),
            pltpu.VMEM((4, 8, 256), F32),
            pltpu.VMEM((3, 1024, 256), BF16),
            pltpu.VMEM((1, 2048), F32),
            pltpu.VMEM((256, 1024), BF16),
            pltpu.VMEM((16, HALF, 128), BF16),
            pltpu.VMEM((4096, 128), BF16),
            pltpu.VMEM((16, HALF, 128), BF16),
            pltpu.VMEM((512, 512), BF16),
            pltpu.VMEM((2048, 128), BF16),
            pltpu.VMEM((128, 2048), BF16),
            pltpu.VMEM((128, 4096), BF16),
            pltpu.VMEM((16, HALF, 128), BF16),
            pltpu.VMEM((16, HALF, 128), BF16),
            pltpu.VMEM((4, 128, 1024), BF16),
            pltpu.VMEM((2, 128, 1024), BF16),
            pltpu.VMEM((128, 1024), BF16),
            pltpu.VMEM((4, 128, 1024), BF16),
            *swap_sems(5),
            *([pltpu.SemaphoreType.DMA((2, 16))] * 2),
            pltpu.SemaphoreType.DMA((7,)),
            *(TEAM_SEMS * 4),
            *COLUMN_SEMS,
        ],
        compiler_params=pltpu.CompilerParams(
            collective_id=1, has_side_effects=True, vmem_limit_bytes=VMEM_LIMIT
        ),
    )(*args)


def backward_kernel(
    second_ref, dy_ref, expand_ref, contract_ref, wo_ref, mixed_ref, resid_ref, bias_ref, params_ref,
    q_ref, kv_ref, wide_ref, lse_ref, first_in_ref, w_ref, x_ref,
    block_out, input_grad_ref, small_out, qkv_out, expand_out, contract_out, output_out,
    act, grad_pre, right, part, near, far, branch, sums_small,
    rows, turned, kv_turned, grad_rows, grad_turned, sums, packed, grad_mine, dq_mine, dkv_mine, dkv_in,
    big, stage, big_last, stage_last, dq_parts, dkv_parts,
    gq, gk, gv, qkv, qkv_stage, norm_send, norm_in, small_steps, small_in,
    swap_send, swap_recv, swap_local, big_local, big_send, big_recv, all_send, all_recv,
    half_send, half_recv, full_send, full_recv, small_send, small_recv, pair_send, pair_recv,
    *team_sems,
):
    place = Place()
    plane, pair, team = Plane(place), Pair(place), Team(place)
    column, cube = Column(place), Cube(place)
    half = query_half(place)
    sequence = place.spot // 4

    def swap(k, group, src, dst):
        return Swap(group, src, dst, swap_send.at[k], swap_recv.at[k], swap_local.at[k])

    def fold(k):
        return Fold(team, part.at[k], near.at[k], far.at[k], team_sems[2 * k], team_sems[2 * k + 1])

    meet([plane, pair, team, column])

    second_fold = fold(0)

    def make(t):
        pre = matmul(second_ref[t], expand_ref[...]) + bias_ref[...]
        value, slope = gelu_both(pre)
        act[t] = value.astype(BF16)
        grad = (matmul_nt(dy_ref[t], contract_ref[...]) * slope).astype(BF16)
        grad_pre[t] = grad
        part[0, t] = matmul_nt(grad, expand_ref[...]).astype(BF16)

    second_fold.send(make)

    def turn(src):
        for t in range(4):
            for at in range(0, src.shape[2], 256):
                right[pl.ds(at, 256), pl.ds(t * 128, 128)] = src[t, :, pl.ds(at, 256)].astype(F32).T.astype(BF16)

    def weight_grad(count, other, put):
        for at in range(0, count, 256):
            left = right[pl.ds(at, 256), :]
            total = matmul(left[:, :128], other[0])
            for t in range(1, 4):
                total = total + matmul(left[:, t * 128 : t * 128 + 128], other[t])
            put(at, total.astype(BF16))

    def bias_grad(row, src):
        total = jnp.sum(src[0].astype(F32), axis=0, keepdims=True)
        for t in range(1, 4):
            total = total + jnp.sum(src[t].astype(F32), axis=0, keepdims=True)
        sums_small[pl.ds(row, 1), :] = total

    halving = Halving(
        big_parts(cube),
        [big.at[k] for k in range(4)] + [big_last],
        [stage.at[k] for k in range(4)] + [stage_last],
        big_send, big_recv,
    )

    def put_contract(at, value):
        big[2 + at // 512, pl.ds(at % 512, 256), :] = value

    def put_expand(at, value):
        big[at // 512, pl.ds(at % 512, 256), :] = value

    def put_output(at, value):
        big_last[pl.ds(0, 256), :] = value[:, :512]
        big_last[pl.ds(256, 256), :] = value[:, 512:]

    turn(act)
    weight_grad(1024, dy_ref, put_contract)
    halving.send(0, (2, 3))
    bias_grad(1, dy_ref)
    bias_grad(2, grad_pre)
    grad_second = second_fold.total()
    gain = params_ref[pl.ds(2, 1), :]
    _, unit, inverse = norm_parts(resid_ref[...], gain, 0.0)
    grad_resid = dy_ref[place.shard].astype(F32) + norm_back(grad_second, unit, inverse, gain)
    sums_small[pl.ds(8, 1), :] = jnp.sum(grad_second * unit, axis=0, keepdims=True)
    sums_small[pl.ds(9, 1), :] = jnp.sum(grad_second, axis=0, keepdims=True)
    branch[place.shard] = grad_resid.astype(BF16)
    share = Share(team, branch, branch.at[place.shard], *team_sems[6:8])
    share.send()
    turn(second_ref)
    weight_grad(1024, grad_pre, put_expand)
    halving.send(0, (0, 1))
    share.forward()
    spread_rows(q_ref, rows, False, 0.125)
    turn_rows(rows, turned, 2048)
    turn_rows(kv_ref, kv_turned, 4096)
    for at in range(0, 4096, TILE):
        sums[pl.ds(at, TILE), :] = jnp.zeros((TILE, 128), F32)
    share.take()
    for t in range(4):
        grad_mixed = matmul_nt(branch[t], wo_ref[...]).astype(BF16)
        for two in range(2):
            lanes = slice(two * 128, two * 128 + 128)
            at = t * 4 + two * 2
            packed[at], packed[at + 1] = swap_heads(grad_mixed[:HALF, lanes], grad_mixed[HALF:, lanes])
    to_heads = swap(0, plane, lambda t: packed.at[t], lambda j, t: grad_mine.at[j])
    to_heads.send_all()
    for t in range(4):
        right[pl.ds(0, 256), pl.ds(t * 128, 128)] = mixed_ref[pl.ds(t * 128, 128), :].astype(F32).T.astype(BF16)
    weight_grad(256, branch, put_output)
    halving.send(0, (4,))
    ffn_fold = fold(1)

    def make_ffn(t):
        part[1, t] = matmul(act[t], contract_ref[...]).astype(BF16)

    ffn_fold.send(make_ffn)
    bias_grad(0, branch)

    dq = swap(1, plane, lambda t: dq_mine.at[t], lambda j, t: dq_parts.at[j])
    dkv = [
        swap(
            2 + k, plane,
            lambda t, k=k: dkv_mine.at[kv_place(half_of(place.layer) * 16 + t, k == 0)],
            lambda j, t, k=k: kv_block(dkv_parts, j, k == 0),
        )
        for k in range(2)
    ]

    def half_of(layer):
        return (layer + place.shard // 2 + sequence // 2) % 2

    def piece_rows(layer, k):
        start = half_of(layer) * 1024
        start = (3072 - start if k >= 2 else start) + (k % 2) * TILE
        return pl.ds(pl.multiple_of(start, TILE), TILE)

    def give(k):
        return pltpu.make_async_remote_copy(
            src_ref=dkv_mine.at[piece_rows(1 - place.layer, k)],
            dst_ref=dkv_in.at[k],
            send_sem=pair_send.at[k],
            recv_sem=pair_recv.at[k],
            device_id=pair.device(1 - place.layer),
            device_id_type=MESH,
        )

    to_heads.take_all()
    spread_rows(grad_mine, grad_rows, True, 1.0)
    turn_rows(grad_rows, grad_turned, 2048)
    for number, tile in enumerate((0, 3, 1, 2)):
        cols = pl.ds(tile * TILE, TILE)
        last = tile_place(half, tile)
        delta = jnp.sum(grad_turned[HALF:, cols].astype(F32) * wide_ref[:, cols], axis=0, keepdims=True)
        lse = lse_ref[:, cols]

        def step(kt, accum, masked):
            kv = kv_ref[key_rows(kt), :]
            scores = matmul(kv, turned[:, cols])
            if masked:
                scores = hide_later(scores)
            probs = jnp.exp(scores - lse)
            grad_probs = matmul(kv, grad_turned[:, cols])
            grad_scores = (probs * (grad_probs - delta)).astype(BF16)
            sums[key_rows(kt), :] += matmul(probs.astype(BF16), grad_rows[cols, :]) + matmul(
                grad_scores, rows[cols, :]
            )
            return accum + matmul(kv_turned[:HALF, key_rows(kt)], grad_scores)

        accum = lax.fori_loop(
            0, last, lambda kt, c: step(kt, c, False), jnp.zeros((HALF, TILE), F32)
        )
        accum = step(last, accum, True)
        pack_rows(accum * 0.125, dq_mine, tile)
        if number < 3:
            halving.add(number)
            halving.send(number + 1)
    for k in range(4):
        theirs = piece_rows(1 - place.layer, k)
        dkv_mine[theirs, :] = sums[theirs, :].astype(BF16)
        give(k).start()
    dq.send_all()
    halving.add(3)
    halving.send(4)
    for k in range(4):
        mine = piece_rows(place.layer, k)
        give(k).wait_recv()
        dkv_mine[mine, :] = (sums[mine, :] + dkv_in[k].astype(F32)).astype(BF16)
        for block in range(8):
            spot = (k % 2) * 8 + block if k < 2 else 15 - ((k % 2) * 8 + block)

            @pl.when(spot != plane.me)
            def _(spot=spot, k=k):
                dkv[k // 2].copy(spot).start()

    for item in dkv:
        item.own().start()
    halving.add(4)
    outs = [expand_out.at[0], expand_out.at[1], contract_out.at[0], contract_out.at[1], output_out]
    gather = Doubling(halving.parts, outs, all_send, all_recv)
    starts = [
        pltpu.make_async_copy(
            piece.view(halving.buffers[k], piece.held[5]), piece.view(outs[k], piece.held[5]), big_local.at[k]
        )
        for k, piece in enumerate(gather.parts)
    ]
    for start in starts:
        start.start()
    block_out[...] = (resid_ref[...] + ffn_fold.total() + params_ref[pl.ds(5, 1), :]).astype(BF16)
    for at in range(0, 1024, 256):
        right[pl.ds(at, 256), :] = first_in_ref[:, pl.ds(at, 256)].astype(F32).T.astype(BF16)
    for start in starts:
        start.wait()
    gather.send(3)

    parts = [Part(cube, 2 * k, 256, 16) for k in range(3)]
    qkv_halving = Halving(
        parts, [qkv.at[k] for k in range(3)], [qkv_stage.at[k] for k in range(3)], half_send, half_recv
    )

    def projection_grad(k, grad):
        for f in range(4):
            qkv[k, :, pl.ds(f * 256, 256)] = matmul(right[pl.ds(f * 256, 256), :], grad[...]).astype(BF16)
        qkv_halving.send(0, (k,))

    dq.take_all()
    unpack_into(gq, dq_parts)
    projection_grad(0, gq)
    for item in dkv:
        item.take_all()
    for at in range(0, 512, 128):
        here = pl.ds(at, 128)
        for two in range(2):
            lanes = pl.ds(two * 128, 128)
            gk[here, lanes], gv[here, lanes] = swap_heads(
                dkv_parts[here, two * 256 : two * 256 + 128], dkv_parts[here, two * 256 + 128 : two * 256 + 256]
            )
    projection_grad(1, gk)
    projection_grad(2, gv)
    first_fold = fold(2)

    def make_first(t):
        here = pl.ds(pl.multiple_of(t * 128, 128), 128)
        part[2, t] = (
            matmul_nt(gq[here, :], w_ref[0])
            + matmul_nt(gk[here, :], w_ref[1])
            + matmul_nt(gv[here, :], w_ref[2])
        ).astype(BF16)

    first_fold.send(make_first)
    for step in range(2):
        gather.take(3 - step)
        gather.send(2 - step)
        qkv_halving.add(step)
        qkv_halving.send(step + 1)
    grad_first = first_fold.total()
    gain = params_ref[pl.ds(0, 1), :]
    _, unit, inverse = norm_parts(x_ref[...].astype(F32), gain, 0.0)
    input_grad_ref[...] = (grad_resid + norm_back(grad_first, unit, inverse, gain)).astype(BF16)
    norm_rows = [
        jnp.sum(grad_first * unit, axis=0, keepdims=True),
        jnp.sum(grad_first, axis=0, keepdims=True),
    ]
    norm_send[...] = jnp.zeros_like(norm_send)
    for t in range(4):
        for k in range(2):
            norm_send[t, pl.ds(k, 1), :] = norm_rows[k][:, t * 256 : t * 256 + 256]
            norm_send[t, pl.ds(2 + k, 1), :] = sums_small[pl.ds(8 + k, 1), pl.ds(t * 256, 256)]
    to_column = swap(4, column, lambda t: norm_send.at[t], lambda j, t: norm_in.at[j])
    to_column.send_all()
    for step in range(2, 5):
        if step == 2:
            gather.take(1)
            gather.send(0)
        qkv_halving.add(step)
        if step < 4:
            qkv_halving.send(step + 1)
    cross = []
    for k, piece in enumerate(parts):
        row, _ = piece.held[5]

        def block(ref, f, row=row):
            return ref.at[
                pl.ds(pl.multiple_of(row, 16), 16), pl.ds(pl.multiple_of(f * 256, 256), 256)
            ]

        cross.append(swap(
            5 + k, column,
            lambda t, k=k, block=block: block(qkv.at[k], t),
            lambda j, t, k=k, block=block: block(qkv_out.at[k], j),
        ))
    for item in cross:
        item.send_all()
    to_column.take_all()
    small = small_steps.at[0]
    small[pl.ds(0, 8), :] = norm_in[0] + norm_in[1] + norm_in[2] + norm_in[3]
    small[pl.ds(4, 1), :] = jnp.sum(gq[...].astype(F32), axis=0, keepdims=True)
    small[pl.ds(5, 1), :] = jnp.sum(gv[...].astype(F32), axis=0, keepdims=True)
    own_lanes = pl.ds(pl.multiple_of(place.shard * 256, 256), 256)
    small[pl.ds(6, 1), :] = sums_small[pl.ds(0, 1), own_lanes]
    small[pl.ds(7, 1), :] = sums_small[pl.ds(1, 1), own_lanes]
    small[pl.ds(8, 8), :] = jnp.zeros((8, 256), F32)
    for t in range(4):
        small[pl.ds(8 + t, 1), :] = sums_small[pl.ds(2, 1), pl.ds(t * 256, 256)]
    full = Doubling(parts, [qkv_out.at[k] for k in range(3)], full_send, full_recv)

    def small_copy(step):
        return pltpu.make_async_remote_copy(
            src_ref=small_steps.at[step],
            dst_ref=small_in.at[step],
            send_sem=small_send.at[step],
            recv_sem=small_recv.at[step],
            device_id=cube.device(step),
            device_id_type=MESH,
        )

    small_copy(0).start()
    for item in cross:
        item.take_all()
    for step in range(5):
        if step > 0:
            full.send(4 - step)
            small_copy(step).start()
            full.take(4 - step)
        small_copy(step).wait_recv()
        small_steps[step + 1] = small_steps[step] + small_in[step]
    small_out[...] = small_steps[5]
    gather.take(0)
    for item in [to_heads, dq, *dkv, to_column, *cross]:
        item.sent_all()
    for item in (second_fold, ffn_fold, first_fold, share):
        item.sent()
    for item in (halving, gather, qkv_halving, full):
        item.finish()
    for k in range(4):
        give(k).wait_send()
    for step in range(5):
        small_copy(step).wait_send()


def backward(*args):
    vmem = pl.BlockSpec(memory_space=pltpu.VMEM)
    anywhere = pl.BlockSpec(memory_space=pl.ANY)
    blocks = pltpu.VMEM((4, 128, 1024), BF16)
    heads = pltpu.VMEM((16, HALF, 128), BF16)
    return pl.pallas_call(
        backward_kernel,
        name="backward",
        out_shape=[
            jax.ShapeDtypeStruct((128, 1024), BF16),
            jax.ShapeDtypeStruct((128, 1024), BF16),
            jax.ShapeDtypeStruct((16, 256), F32),
            jax.ShapeDtypeStruct((3, 256, 1024), BF16),
            jax.ShapeDtypeStruct((2, 512, 1024), BF16),
            jax.ShapeDtypeStruct((2, 512, 1024), BF16),
            jax.ShapeDtypeStruct((512, 512), BF16),
        ],
        in_specs=[vmem] * len(args),
        out_specs=[vmem] * 3 + [anywhere] * 4,
        scratch_shapes=[
            blocks,
            blocks,
            pltpu.VMEM((1024, 512), BF16),
            pltpu.VMEM((3, 4, 128, 1024), BF16),
            pltpu.VMEM((3, 2, 128, 1024), BF16),
            pltpu.VMEM((3, 128, 1024), BF16),
            blocks,
            pltpu.VMEM((16, 1024), F32),
            pltpu.VMEM((2048, 128), BF16),
            pltpu.VMEM((128, 2048), BF16),
            pltpu.VMEM((128, 4096), BF16),
            pltpu.VMEM((2048, 128), BF16),
            pltpu.VMEM((128, 2048), BF16),
            pltpu.VMEM((4096, 128), F32),
            heads,
            heads,
            heads,
            pltpu.VMEM((4096, 128), BF16),
            pltpu.VMEM((4, TILE, 128), BF16),
            pltpu.VMEM((4, 512, 1024), BF16),
            pltpu.VMEM((4, 512, 1024), BF16),
            pltpu.VMEM((512, 512), BF16),
            pltpu.VMEM((512, 512), BF16),
            heads,
            pltpu.VMEM((512, 512), BF16),
            pltpu.VMEM((512, 256), BF16),
            pltpu.VMEM((512, 256), BF16),
            pltpu.VMEM((512, 256), BF16),
            pltpu.VMEM((3, 256, 1024), BF16),
            pltpu.VMEM((3, 256, 1024), BF16),
            pltpu.VMEM((4, 8, 256), F32),
            pltpu.VMEM((4, 8, 256), F32),
            pltpu.VMEM((6, 16, 256), F32),
            pltpu.VMEM((5, 16, 256), F32),
            *swap_sems(8),
            pltpu.SemaphoreType.DMA((5,)),
            *([pltpu.SemaphoreType.DMA((5, 5))] * 4),
            *([pltpu.SemaphoreType.DMA((3, 5))] * 4),
            *([pltpu.SemaphoreType.DMA((5,))] * 2),
            *([pltpu.SemaphoreType.DMA((4,))] * 2),
            *(TEAM_SEMS * 4),
        ],
        compiler_params=pltpu.CompilerParams(
            collective_id=2, has_side_effects=True, vmem_limit_bytes=VMEM_LIMIT
        ),
    )(*args)


def on_device(
    tokens, query_weight, key_weight, value_weight, output_weight, expand_weight, contract_weight,
    query_bias, value_bias, output_bias, expand_bias, contract_bias,
    first_gain, first_shift, second_gain, second_shift, cotangent,
):
    vectors = [
        first_gain, first_shift, second_gain, second_shift, output_bias, contract_bias, query_bias, value_bias
    ]
    vectors = jnp.concatenate(vectors).astype(F32).reshape(8, 256)
    first_in, mixed, resid, wide, lse, params, q_mine, kv_mine, dy_all, second_in, weights = forward(
        vectors, tokens[0], output_weight, cotangent[0], query_weight, key_weight, value_weight
    )
    block_output, input_grad, small, qkv, expand, contract, output = backward(
        second_in, dy_all, expand_weight, contract_weight, output_weight, mixed, resid,
        expand_bias[None].astype(F32), params,
        q_mine, kv_mine, wide, lse, first_in, weights, tokens[0],
    )
    return (
        block_output[None],
        input_grad[None],
        qkv[0].astype(F32),
        qkv[1].astype(F32),
        qkv[2].astype(F32),
        jnp.concatenate([output[:256], output[256:]], axis=1).astype(F32),
        expand.reshape(1024, 1024).astype(F32),
        contract.reshape(1024, 1024).astype(F32),
        small[4],
        small[5],
        small[6],
        small[8:12].reshape(1024),
        small[7],
        small[0],
        small[1],
        small[2],
        small[3],
    )


def solution(mesh):
    weights = [P("fsdp", None)] * 4 + [P(None, "fsdp"), P("fsdp", None)]
    rows = P("fsdp", "seq", None)
    return jax.shard_map(
        on_device,
        mesh=mesh,
        in_specs=(rows, *weights, *([P("fsdp")] * 9), rows),
        out_specs=(rows, rows, *weights, *([P("fsdp")] * 9)),
        check_vma=False,
    )
```

```python
import functools

import jax
import jax.numpy as jnp
from jax import lax
from jax.experimental import pallas as pl
from jax.experimental.pallas import tpu as pltpu
from jax.sharding import PartitionSpec as P

MESH = pl.DeviceIdType.MESH
BF16 = jnp.bfloat16
F32 = jnp.float32
TILE = 512
HALF = 64
VMEM_LIMIT = 60 * 1024 * 1024


def matmul(left, right):
    return jnp.dot(left, right, preferred_element_type=F32)


def matmul_tn(left, right):
    return lax.dot_general(left, right, (((0,), (0,)), ((), ())), preferred_element_type=F32)


def matmul_nt(left, right):
    return lax.dot_general(left, right, (((1,), (1,)), ((), ())), preferred_element_type=F32)


def norm_parts(values, gain, shift):
    mean = jnp.mean(values, axis=-1, keepdims=True)
    centered = values - mean
    variance = jnp.mean(centered * centered, axis=-1, keepdims=True)
    inverse = lax.rsqrt(variance + 1e-05)
    normed = centered * inverse
    return (normed * gain + shift, normed, inverse)


def norm_back(grad, normed, inverse, gain):
    scaled = grad * gain
    return inverse * (
        scaled
        - jnp.mean(scaled, axis=-1, keepdims=True)
        - normed * jnp.mean(scaled * normed, axis=-1, keepdims=True)
    )


def gelu_both(values):
    square = values * values
    inner = jnp.tanh(0.7978845608028654 * (values + 0.044715 * square * values))
    value = 0.5 * values * (1.0 + inner)
    slope = 0.5 * (1.0 + inner) + 0.5 * values * (1.0 - inner * inner) * 0.7978845608028654 * (
        1.0 + 0.134145 * square
    )
    return value, slope


class Place:
    def __init__(self):
        self.seq = lax.axis_index("seq")
        self.shard = lax.axis_index("fsdp")
        self.layer = self.seq // 16
        self.spot = self.seq % 16
        self.team = (self.layer + self.shard // 2) % 2


class Team:
    size = 4

    def __init__(self, place):
        self.place = place
        self.me = place.shard

    def device(self, t):
        return {"seq": ((self.place.team + t // 2) % 2) * 16 + self.place.spot, "fsdp": t}


class Plane:
    size = 16

    def __init__(self, place):
        self.place = place
        self.me = place.spot

    def device(self, t):
        return {"seq": self.place.layer * 16 + t, "fsdp": self.place.shard}


class Line:
    size = 32

    def __init__(self, place):
        self.place = place
        self.me = place.seq

    def device(self, t):
        return {"seq": t, "fsdp": self.place.shard}


def spread(count, body):
    if count <= 4:
        for step in range(count):
            body(step)
    else:
        lax.fori_loop(0, count, lambda step, c: (body(step), c)[1], 0)


def query_half(place):
    return (place.layer + place.shard // 2 + place.spot // 8) % 2


def tile_place(half, tile):
    return half * 2 + tile if tile < 2 else 6 - 2 * half + tile - 2


def spread_rows(src_ref, out_ref, at_high, factor):
    lane = lax.broadcasted_iota(jnp.int32, (HALF, 128), 1)
    keep = (lane >= HALF) if at_high else (lane < HALF)
    for block in range(16):
        both = src_ref[block].astype(F32) * factor
        moved = pltpu.roll(both, HALF, 1)
        low, high = (moved, both) if at_high else (both, moved)
        out_ref[pl.ds(block * HALF, HALF), :] = jnp.where(keep, low, 0.0).astype(BF16)
        out_ref[pl.ds(1024 + (15 - block) * HALF, HALF), :] = jnp.where(keep, high, 0.0).astype(BF16)


def turn_rows(src_ref, out_ref, rows):
    for at in range(0, rows, TILE):
        out_ref[:, pl.ds(at, TILE)] = src_ref[pl.ds(at, TILE), :].astype(F32).T.astype(BF16)


def pack_rows(turned, out_ref, tile):
    empty = jnp.zeros_like(turned)
    if tile < 2:
        rows = jnp.concatenate([turned, empty], axis=0).T.astype(BF16)
        for part in range(8):
            out_ref[tile * 8 + part] = rows[part * HALF : (part + 1) * HALF]
    else:
        rows = jnp.concatenate([empty, turned], axis=0).T.astype(BF16)
        for part in range(8):
            block = 15 - ((tile - 2) * 8 + part)
            out_ref[block] = out_ref[block] + rows[part * HALF : (part + 1) * HALF]


def key_rows(kt):
    return pl.ds(pl.multiple_of(kt * TILE, TILE), TILE)


def other_tiles(half, tile):
    if tile < 2:
        return 2 - 2 * half, 2
    return 2 - 2 * half, 6 - 4 * half


def hide_later(scores):
    key = lax.broadcasted_iota(jnp.int32, (TILE, TILE), 0)
    query = lax.broadcasted_iota(jnp.int32, (TILE, TILE), 1)
    return jnp.where(key <= query, scores, -1e30)


def stored_block(sender_team, spot, sequence):
    return ((sender_team + sequence // 2) % 2) * 16 + spot


def swap_heads(low, high):
    low, high = low.astype(F32), high.astype(F32)
    left = lax.broadcasted_iota(jnp.int32, low.shape, 1) < HALF
    one = jnp.where(left, low, pltpu.roll(high, HALF, 1))
    two = jnp.where(left, pltpu.roll(low, HALF, 1), high)
    return one.astype(BF16), two.astype(BF16)


def head_pieces(sequence, pair):
    low = pl.ds(sequence * 128, HALF)
    high = pl.ds(sequence * 128 + HALF, HALF)
    lanes = pl.ds(pair * 128, 128)
    return (low, lanes), (high, lanes), sequence * 4 + pair * 2


def pack_into(out_ref, src_ref):
    for sequence in range(4):
        for pair in range(2):
            low, high, at = head_pieces(sequence, pair)
            out_ref[at], out_ref[at + 1] = swap_heads(src_ref[low], src_ref[high])


def unpack_into(out_ref, src_ref):
    for sequence in range(4):
        for pair in range(2):
            low, high, at = head_pieces(sequence, pair)
            out_ref[low], out_ref[high] = swap_heads(src_ref[at], src_ref[at + 1])


def kv_block(ref, spot, low):
    rows = pl.ds(pl.multiple_of((spot // 4) * 128 + (0 if low else HALF), HALF), HALF)
    return ref.at[rows, pl.ds(pl.multiple_of((spot % 4) * 128, 128), 128)]


def kv_place(block, low):
    return pl.ds(pl.multiple_of((block if low else 63 - block) * HALF, HALF), HALF)


class Column:
    size = 4

    def __init__(self, place):
        self.place = place
        self.me = place.shard

    def device(self, t):
        return {"seq": self.place.seq, "fsdp": t}


class Cube:
    def __init__(self, place):
        x, z = place.spot // 4, place.spot % 4
        self.shard = place.shard
        self.bits = [(x + x // 2) % 2, x // 2, (z + z // 2) % 2, z // 2, place.layer]

        def at(x, z, layer):
            return layer * 16 + x * 4 + z

        self.partners = [
            at(x + 1 - 2 * (x % 2), z, place.layer),
            at(3 - x, z, place.layer),
            at(x, z + 1 - 2 * (z % 2), place.layer),
            at(x, 3 - z, place.layer),
            at(x, z, 1 - place.layer),
        ]

    def device(self, bit):
        return {"seq": self.partners[bit], "fsdp": self.shard}


class Part:
    def __init__(self, cube, index, rows, least):
        self.cube = cube
        self.order = [(index + s) % 5 for s in range(5)]
        row = 0
        self.sent, self.held, self.halves = [], [(0, rows)], []
        for bit in self.order:
            value = cube.bits[bit]
            self.halves.append(rows > least)
            if rows > least:
                rows //= 2
                self.sent.append((row + (1 - value) * rows, rows))
                row = row + value * rows
            else:
                self.sent.append((row, rows))
            self.held.append((row, rows))

    def view(self, ref, region):
        row, rows = region
        return ref.at[pl.ds(row if isinstance(row, int) else pl.multiple_of(row, 16), rows)]

    def stage(self, step):
        rows = self.sent[step][1]
        return (rows if self.halves[step] else 0, rows)


class Halving:
    def __init__(self, parts, buffers, stages, send_sem, recv_sem):
        self.parts, self.buffers, self.stages = parts, buffers, stages
        self.send_sem, self.recv_sem = send_sem, recv_sem

    def copy(self, k, step):
        part = self.parts[k]
        return pltpu.make_async_remote_copy(
            src_ref=part.view(self.buffers[k], part.sent[step]),
            dst_ref=part.view(self.stages[k], part.stage(step)),
            send_sem=self.send_sem.at[k, step],
            recv_sem=self.recv_sem.at[k, step],
            device_id=part.cube.device(part.order[step]),
            device_id_type=MESH,
        )

    def send(self, step, which=None):
        for k in which or range(len(self.parts)):
            self.copy(k, step).start()

    def add(self, step):
        for k, part in enumerate(self.parts):
            self.copy(k, step).wait_recv()
            if not part.halves[step]:
                self.copy(k, step).wait_send()
            mine = part.view(self.buffers[k], part.held[step + 1])
            other = part.view(self.stages[k], part.stage(step))
            rows = part.held[step + 1][1]

            def slab(at, c, mine=mine, other=other):
                here = pl.ds(pl.multiple_of(at * 16, 16), 16)
                mine[here, :] = (mine[here, :].astype(F32) + other[here, :].astype(F32)).astype(BF16)
                return c

            if rows == 16:
                slab(0, 0)
            else:
                lax.fori_loop(0, rows // 16, slab, 0)

    def finish(self):
        for k, part in enumerate(self.parts):
            for step in range(5):
                if part.halves[step]:
                    self.copy(k, step).wait_send()


class Doubling:
    def __init__(self, parts, buffers, send_sem, recv_sem):
        self.parts, self.buffers = parts, buffers
        self.send_sem, self.recv_sem = send_sem, recv_sem

    def copy(self, k, step):
        part = self.parts[k]
        view = part.view(self.buffers[k], part.held[step + 1])
        return pltpu.make_async_remote_copy(
            src_ref=view,
            dst_ref=view,
            send_sem=self.send_sem.at[k, step],
            recv_sem=self.recv_sem.at[k, step],
            device_id=part.cube.device(part.order[step]),
            device_id_type=MESH,
        )

    def landed(self, k, step):
        part = self.parts[k]
        view = part.view(self.buffers[k], part.sent[step])
        return pltpu.make_async_remote_copy(
            src_ref=view,
            dst_ref=view,
            send_sem=self.send_sem.at[k, step],
            recv_sem=self.recv_sem.at[k, step],
            device_id=part.cube.device(part.order[step]),
            device_id_type=MESH,
        )

    def send(self, step):
        for k in range(len(self.parts)):
            self.copy(k, step).start()

    def take(self, step):
        for k in range(len(self.parts)):
            self.landed(k, step).wait_recv()

    def finish(self):
        for k in range(len(self.parts)):
            for step in range(4):
                self.copy(k, step).wait_send()


def big_parts(cube):
    return [Part(cube, k, 512, 32) for k in range(5)]


def meet(groups):
    barrier = pltpu.get_barrier_semaphore()
    for grp in groups:

        def hello(step, grp=grp):
            pl.semaphore_signal(
                barrier, inc=1, device_id=grp.device((grp.me + 1 + step) % grp.size), device_id_type=MESH
            )

        spread(grp.size - 1, hello)
    pl.semaphore_wait(barrier, sum(grp.size - 1 for grp in groups))


class Swap:
    def __init__(self, group, src, dst, send_sem, recv_sem, local_sem):
        self.group, self.src, self.dst = group, src, dst
        self.send_sem, self.recv_sem, self.local_sem = send_sem, recv_sem, local_sem

    def copy(self, target):
        return pltpu.make_async_remote_copy(
            src_ref=self.src(target),
            dst_ref=self.dst(self.group.me, target),
            send_sem=self.send_sem.at[target],
            recv_sem=self.recv_sem.at[self.group.me],
            device_id=self.group.device(target),
            device_id_type=MESH,
        )

    def landed(self, sender):
        view = self.dst(sender, self.group.me)
        return pltpu.make_async_remote_copy(
            src_ref=view,
            dst_ref=view,
            send_sem=self.send_sem.at[sender],
            recv_sem=self.recv_sem.at[sender],
            device_id=self.group.device(sender),
            device_id_type=MESH,
        )

    def own(self):
        return pltpu.make_async_copy(
            self.src(self.group.me), self.dst(self.group.me, self.group.me), self.local_sem
        )

    def send(self, step):
        self.copy((self.group.me + 1 + step) % self.group.size).start()

    def take(self, step):
        self.landed((self.group.me + 1 + step) % self.group.size).wait_recv()

    def sent(self, step):
        self.copy((self.group.me + 1 + step) % self.group.size).wait_send()

    def send_all(self):
        spread(self.group.size - 1, self.send)
        self.own().start()

    def take_all(self):
        spread(self.group.size - 1, self.take)
        self.own().wait()

    def sent_all(self):
        spread(self.group.size - 1, self.sent)


def swap_sems(count):
    return [
        pltpu.SemaphoreType.DMA((count, 32)),
        pltpu.SemaphoreType.DMA((count, 32)),
        pltpu.SemaphoreType.DMA((count,)),
    ]


class Square:
    size = 4

    def __init__(self, place):
        self.place = place
        self.x, self.z = place.spot // 4, place.spot % 4
        self.me = ((self.x + self.x // 2) % 2) * 2 + (self.z + self.z // 2) % 2

    def device(self, t):
        x = 2 * (self.x // 2) + (t // 2 + self.x // 2) % 2
        z = 2 * (self.z // 2) + (t % 2 + self.z // 2) % 2
        return {"seq": self.place.layer * 16 + x * 4 + z, "fsdp": self.place.shard}


class Columns:
    def __init__(self, team, square, sources, out, sems):
        self.team, self.square, self.sources, self.out = team, square, sources, out
        self.near_send, self.near_recv, self.far_send, self.far_recv, self.pass_send, self.pass_recv, self.local = sems
        me = team.me
        self.me = me
        self.sibling = (me // 2) * 2 + 1 - me % 2
        across = (me + 2) % 4
        self.far = (across, (self.sibling + 2) % 4)

    def lanes(self, member):
        return pl.ds(pl.multiple_of(member * 256, 256), 256)

    def block(self, k, member):
        return self.out.at[k, self.lanes(member)]

    def quarter(self, k, member, spot):
        return self.out.at[k, pl.ds(pl.multiple_of(member * 256 + spot * 64, 64), 64)]

    def remote(self, src, dst, send_sem, recv_sem, device):
        return pltpu.make_async_remote_copy(
            src_ref=src, dst_ref=dst, send_sem=send_sem, recv_sem=recv_sem, device_id=device, device_id_type=MESH
        )

    def near(self, k, arriving=False):
        dst = self.block(k, self.sibling if arriving else self.me)
        src = dst if arriving else self.sources[k].at[:, self.lanes(self.sibling)]
        return self.remote(src, dst, self.near_send.at[k], self.near_recv.at[k], self.team.device(self.sibling))

    def far_copy(self, k, which, arriving=False):
        other = self.far[which]
        dst = self.quarter(k, other if arriving else self.me, self.square.me)
        rows = pl.ds(pl.multiple_of(self.square.me * 64, 64), 64)
        src = dst if arriving else self.sources[k].at[rows, self.lanes(other)]
        at = which * 3 + k
        return self.remote(src, dst, self.far_send.at[at], self.far_recv.at[at], self.team.device(other))

    def pass_copy(self, k, which, step, arriving=False):
        spot = (self.square.me + 1 + step) % 4
        view = self.quarter(k, self.far[which], spot if arriving else self.square.me)
        at = which * 3 + k
        return self.remote(
            view, view, self.pass_send.at[at, spot], self.pass_recv.at[at, spot if arriving else self.square.me],
            self.square.device(spot),
        )

    def own(self, k):
        return pltpu.make_async_copy(self.sources[k].at[:, self.lanes(self.me)], self.block(k, self.me), self.local.at[k])

    def send(self):
        for k in range(3):
            for which in range(2):
                self.far_copy(k, which).start()
        for k in range(3):
            self.near(k).start()
            self.own(k).start()

    def forward(self):
        for k in range(3):
            for which in range(2):
                self.far_copy(k, which, True).wait_recv()
                for step in range(3):
                    self.pass_copy(k, which, step).start()

    def take(self):
        for k in range(3):
            self.own(k).wait()
            self.near(k, True).wait_recv()
            for which in range(2):
                for step in range(3):
                    self.pass_copy(k, which, step, True).wait_recv()

    def sent(self):
        for k in range(3):
            self.near(k).wait_send()
            for which in range(2):
                self.far_copy(k, which).wait_send()
                for step in range(3):
                    self.pass_copy(k, which, step).wait_send()


COLUMN_SEMS = [
    *([pltpu.SemaphoreType.DMA((3,))] * 2),
    *([pltpu.SemaphoreType.DMA((6,))] * 2),
    *([pltpu.SemaphoreType.DMA((6, 4))] * 2),
    pltpu.SemaphoreType.DMA((3,)),
]


class Pair:
    size = 2

    def __init__(self, place):
        self.place = place
        self.me = place.layer

    def device(self, t):
        return {"seq": t * 16 + self.place.spot, "fsdp": self.place.shard}


class Fold:
    def __init__(self, team, part, near, far, send_sem, recv_sem):
        self.team, self.part, self.near, self.far = team, part, near, far
        self.send_sem, self.recv_sem = send_sem, recv_sem
        me = team.me
        self.me = me
        self.sibling = (me // 2) * 2 + 1 - me % 2
        self.across = (me + 2) % 4
        self.opposite = (self.sibling + 2) % 4

    def copy(self, k):
        if k < 2:
            src, dst, to = self.part.at[(self.opposite, self.sibling)[k]], self.near.at[k], self.sibling
        else:
            src, dst, to = self.part.at[self.across], self.far, self.across
        return pltpu.make_async_remote_copy(
            src_ref=src,
            dst_ref=dst,
            send_sem=self.send_sem.at[k],
            recv_sem=self.recv_sem.at[k],
            device_id=self.team.device(to),
            device_id_type=MESH,
        )

    def send(self, make):
        make(self.opposite)
        self.copy(0).start()
        make(self.across)
        self.copy(0).wait_recv()
        self.part[self.across] = (
            self.part[self.across].astype(F32) + self.near[0].astype(F32)
        ).astype(BF16)
        self.copy(2).start()
        make(self.sibling)
        self.copy(1).start()
        make(self.me)

    def total(self):
        self.copy(1).wait_recv()
        self.copy(2).wait_recv()
        return self.part[self.me].astype(F32) + self.near[1].astype(F32) + self.far[...].astype(F32)

    def sent(self):
        for k in range(3):
            self.copy(k).wait_send()


class Share:
    def __init__(self, team, out, own, send_sem, recv_sem):
        self.team, self.out, self.own = team, out, own
        self.send_sem, self.recv_sem = send_sem, recv_sem
        me = team.me
        self.me = me
        self.sibling = (me // 2) * 2 + 1 - me % 2
        self.across = (me + 2) % 4
        self.opposite = (self.sibling + 2) % 4

    def rows(self, k):
        return pl.ds((k % 2) * 64, 64)

    def copy(self, k):
        kind = k // 2
        src = self.own.at[self.rows(k)] if kind < 2 else self.out.at[self.across, self.rows(k)]
        block = self.me if kind < 2 else self.across
        return pltpu.make_async_remote_copy(
            src_ref=src,
            dst_ref=self.out.at[block, self.rows(k)],
            send_sem=self.send_sem.at[k],
            recv_sem=self.recv_sem.at[k],
            device_id=self.team.device(self.across if kind == 1 else self.sibling),
            device_id_type=MESH,
        )

    def landed(self, k):
        view = self.out.at[(self.sibling, self.across, self.opposite)[k // 2], self.rows(k)]
        return pltpu.make_async_remote_copy(
            src_ref=view,
            dst_ref=view,
            send_sem=self.send_sem.at[k],
            recv_sem=self.recv_sem.at[k],
            device_id=self.team.device(self.across if k // 2 == 1 else self.sibling),
            device_id_type=MESH,
        )

    def send(self):
        for k in (2, 3, 0, 1):
            self.copy(k).start()

    def forward(self):
        for k in (2, 3):
            self.landed(k).wait_recv()
            self.copy(k + 2).start()

    def take(self):
        for k in (0, 1, 4, 5):
            self.landed(k).wait_recv()

    def sent(self):
        for k in range(6):
            self.copy(k).wait_send()


TEAM_SEMS = [pltpu.SemaphoreType.DMA((6,)), pltpu.SemaphoreType.DMA((6,))]


def forward_kernel(
    vec_ref, x_ref, wo_from, dy_ref, wq_ref, wk_ref, wv_ref,
    first_in_ref, mixed_ref, resid_ref, wide_ref, lse_ref, params_ref, q_out, kv_out, dy_out, second_out, w_out,
    x_all, vec_all, weights, totals, wo_ref,
    q_mine, kv_mine, q_send, kv_send, rows, turned, kv_turned, mixed_mine, mixed_in, part, near, far, second,
    swap_send, swap_recv, swap_local, pass_send, pass_recv, save_sem,
    dy_send, dy_recv, fold_send, fold_recv, share_send, share_recv, x_send, x_recv, *column_sems,
):
    place = Place()
    plane, pair, team = Plane(place), Pair(place), Team(place)
    half = query_half(place)
    sequence = place.spot // 4

    def swap(k, group, src, dst):
        return Swap(group, src, dst, swap_send.at[k], swap_recv.at[k], swap_local.at[k])

    meet([plane, pair, team])
    dy = Share(team, dy_out, dy_ref, dy_send, dy_recv)
    dy_own = pltpu.make_async_copy(dy_ref, dy_out.at[team.me], save_sem.at[0])
    vec = swap(4, team, lambda t: vec_ref, lambda j, t: vec_all.at[j])
    columns = Columns(team, Square(place), (wq_ref, wk_ref, wv_ref), weights, column_sems)
    x = Share(team, x_all, x_ref, x_send, x_recv)
    vec.send_all()
    columns.send()
    x.send()
    dy_own.start()
    x_own = pltpu.make_async_copy(x_ref, x_all.at[team.me], save_sem.at[5])
    load_wo = pltpu.make_async_copy(wo_from, wo_ref, save_sem.at[6])
    x_own.start()
    load_wo.start()
    columns.forward()
    x.forward()
    dy.send()
    vec.take_all()
    for t in range(4):
        params_ref[:, pl.ds(t * 256, 256)] = vec_all[t]
    x.take()
    x_own.wait()
    columns.take()
    save_w = pltpu.make_async_copy(weights, w_out, save_sem.at[4])
    save_w.start()

    def kv_rows(layer, spot, seq, low):
        return kv_place(stored_block((layer + place.shard // 2) % 2, spot, seq), low)

    heads = [
        swap(
            k, plane,
            lambda t, k=k: kv_block(kv_send, t, k == 0),
            lambda j, t, k=k: kv_mine.at[kv_rows(place.layer, j, t // 4, k == 0)],
        )
        for k in range(2)
    ]
    heads.append(swap(2, plane, lambda t: q_send.at[t], lambda j, t: q_mine.at[j]))
    gain, shift = params_ref[pl.ds(0, 1), :], params_ref[pl.ds(1, 1), :]
    for turn in range(4):
        s = (sequence + 1 + turn) % 4
        normed = norm_parts(x_all[s].astype(F32), gain, shift)[0].astype(BF16)
        first_in_ref[pl.ds(pl.multiple_of(s * 128, 128), 128), :] = normed
        query = (matmul(normed, weights[0]) + vec_ref[pl.ds(6, 1), :]).astype(BF16)
        key = matmul(normed, weights[1]).astype(BF16)
        value = (matmul(normed, weights[2]) + vec_ref[pl.ds(7, 1), :]).astype(BF16)
        for two in range(2):
            lanes = slice(two * 128, two * 128 + 128)
            at = s * 4 + two * 2
            for part_of in range(2):
                cut = slice(part_of * HALF, part_of * HALF + HALF)
                one, other = swap_heads(key[cut, lanes], value[cut, lanes])
                down = pl.ds(pl.multiple_of(s * 128 + part_of * HALF, HALF), HALF)
                kv_send[down, two * 256 : two * 256 + 128] = one
                kv_send[down, two * 256 + 128 : two * 256 + 256] = other
            q_send[at], q_send[at + 1] = swap_heads(query[:HALF, lanes], query[HALF:, lanes])
        for head in range(4 if turn < 3 else 3):
            target = s * 4 + (place.spot + 1 + head) % 4
            for item in heads:
                item.copy(target).start()

    for item in heads:
        item.own().start()

    def pass_on(k, j):
        view = kv_mine.at[kv_rows(place.layer, j, sequence, k == 0)]
        return pltpu.make_async_remote_copy(
            src_ref=view,
            dst_ref=view,
            send_sem=pass_send.at[k, j],
            recv_sem=pass_recv.at[k, j],
            device_id=pair.device(1 - place.layer),
            device_id_type=MESH,
        )

    def passed(k, j):
        view = kv_mine.at[kv_rows(1 - place.layer, j, sequence, k == 0)]
        return pltpu.make_async_remote_copy(
            src_ref=view,
            dst_ref=view,
            send_sem=pass_send.at[k, j],
            recv_sem=pass_recv.at[k, j],
            device_id=pair.device(1 - place.layer),
            device_id_type=MESH,
        )

    for item in heads:
        item.own().wait()
    for k in range(2):
        pass_on(k, plane.me).start()

    def relay(step, c):
        j = (plane.me + 15 - step) % 16
        for k in range(2):
            heads[k].landed(j).wait_recv()
            pass_on(k, j).start()
        heads[2].landed(j).wait_recv()
        return c

    lax.fori_loop(0, 15, relay, 0)
    spread_rows(q_mine, rows, False, 0.125)
    turn_rows(rows, turned, 2048)

    def turn_keys(kt):
        kv_turned[:, key_rows(kt)] = kv_mine[key_rows(kt), :].astype(F32).T.astype(BF16)

    def step(kt, carry, cols, masked):
        top, total, accum = carry
        scores = matmul(kv_mine[key_rows(kt), :], turned[:, cols])
        if masked:
            scores = hide_later(scores)
        new_top = jnp.maximum(top, jnp.max(scores, axis=0, keepdims=True))
        probs = jnp.exp(scores - new_top)
        fade = jnp.exp(top - new_top)
        total = total * fade + jnp.sum(probs, axis=0, keepdims=True)
        accum = accum * fade + matmul(kv_turned[HALF:, key_rows(kt)], probs.astype(BF16))
        return new_top, total, accum

    for tile in range(4):
        turn_keys(tile_place(half, tile))
    for tile in range(4):
        cols = pl.ds(tile * TILE, TILE)
        carry = (
            jnp.full((1, TILE), -1e30, F32),
            jnp.zeros((1, TILE), F32),
            jnp.zeros((HALF, TILE), F32),
        )
        for before in range(tile + 1):
            carry = step(tile_place(half, before), carry, cols, before == tile)
        lse_ref[:, cols], totals[:, cols], wide_ref[:, cols] = carry

    def arrive(j, c):
        for k in range(2):
            passed(k, j).wait_recv()
        return c

    lax.fori_loop(0, 16, arrive, 0)
    saves = [
        pltpu.make_async_copy(q_mine, q_out, save_sem.at[1]),
        pltpu.make_async_copy(kv_mine, kv_out, save_sem.at[2]),
    ]
    for save in saves:
        save.start()
    dy.forward()
    for tile in range(4):
        turn_keys(tile_place(1 - half, tile))
    mix = swap(3, plane, lambda t: mixed_mine.at[t], lambda j, t: mixed_in.at[j])
    for number, tile in enumerate((0, 3, 1, 2)):
        cols = pl.ds(tile * TILE, TILE)
        low, high = other_tiles(half, tile)
        top, total, accum = lax.fori_loop(
            low, high, lambda kt, c: step(kt, c, cols, False), (lse_ref[:, cols], totals[:, cols], wide_ref[:, cols])
        )
        wide = accum * (1.0 / total)
        wide_ref[:, cols] = wide
        lse_ref[:, cols] = top + jnp.log(total)
        pack_rows(wide, mixed_mine, tile)
        if number % 2:
            for target in range(4 * (number - 1), 4 * (number - 1) + 8):

                @pl.when(target != plane.me)
                def _(target=target):
                    mix.copy(target).start()

    mix.own().start()
    mix.take_all()
    unpack_into(mixed_ref, mixed_in)
    fold = Fold(team, part, near, far, fold_send, fold_recv)
    load_wo.wait()

    def branch(t):
        here = pl.ds(pl.multiple_of(t * 128, 128), 128)
        part[t] = matmul(mixed_ref[here, :], wo_ref[...]).astype(BF16)

    fold.send(branch)
    resid = x_all[place.shard].astype(F32) + fold.total() + params_ref[pl.ds(4, 1), :]
    resid_ref[...] = resid
    second[place.shard] = norm_parts(resid, params_ref[pl.ds(2, 1), :], params_ref[pl.ds(3, 1), :])[0].astype(BF16)
    share = Share(team, second, second.at[place.shard], share_send, share_recv)
    share.send()
    share.forward()
    dy.take()
    share.take()
    save_second = pltpu.make_async_copy(second, second_out, save_sem.at[3])
    save_second.start()
    for save in saves:
        save.wait()
    dy_own.wait()
    dy.sent()
    for item in heads:
        item.sent_all()

    def gone(j, c):
        for k in range(2):
            pass_on(k, j).wait_send()
        return c

    lax.fori_loop(0, 16, gone, 0)
    mix.sent_all()
    fold.sent()
    share.sent()
    save_second.wait()
    save_w.wait()
    vec.sent_all()
    columns.sent()
    x.sent()


def forward(*args):
    vmem = pl.BlockSpec(memory_space=pltpu.VMEM)
    anywhere = pl.BlockSpec(memory_space=pl.ANY)
    return pl.pallas_call(
        forward_kernel,
        name="forward",
        out_shape=[
            jax.ShapeDtypeStruct((512, 1024), BF16),
            jax.ShapeDtypeStruct((512, 256), BF16),
            jax.ShapeDtypeStruct((128, 1024), F32),
            jax.ShapeDtypeStruct((HALF, 2048), F32),
            jax.ShapeDtypeStruct((1, 2048), F32),
            jax.ShapeDtypeStruct((8, 1024), F32),
            jax.ShapeDtypeStruct((16, HALF, 128), BF16),
            jax.ShapeDtypeStruct((4096, 128), BF16),
            jax.ShapeDtypeStruct((4, 128, 1024), BF16),
            jax.ShapeDtypeStruct((4, 128, 1024), BF16),
            jax.ShapeDtypeStruct((3, 1024, 256), BF16),
        ],
        in_specs=[vmem] + [anywhere] * 6,
        out_specs=[vmem] * 6 + [anywhere] * 5,
        scratch_shapes=[
            pltpu.VMEM((4, 128, 1024), BF16),
            pltpu.VMEM((4, 8, 256), F32),
            pltpu.VMEM((3, 1024, 256), BF16),
            pltpu.VMEM((1, 2048), F32),
            pltpu.VMEM((256, 1024), BF16),
            pltpu.VMEM((16, HALF, 128), BF16),
            pltpu.VMEM((4096, 128), BF16),
            pltpu.VMEM((16, HALF, 128), BF16),
            pltpu.VMEM((512, 512), BF16),
            pltpu.VMEM((2048, 128), BF16),
            pltpu.VMEM((128, 2048), BF16),
            pltpu.VMEM((128, 4096), BF16),
            pltpu.VMEM((16, HALF, 128), BF16),
            pltpu.VMEM((16, HALF, 128), BF16),
            pltpu.VMEM((4, 128, 1024), BF16),
            pltpu.VMEM((2, 128, 1024), BF16),
            pltpu.VMEM((128, 1024), BF16),
            pltpu.VMEM((4, 128, 1024), BF16),
            *swap_sems(5),
            *([pltpu.SemaphoreType.DMA((2, 16))] * 2),
            pltpu.SemaphoreType.DMA((7,)),
            *(TEAM_SEMS * 4),
            *COLUMN_SEMS,
        ],
        compiler_params=pltpu.CompilerParams(
            collective_id=1, has_side_effects=True, vmem_limit_bytes=VMEM_LIMIT
        ),
    )(*args)


def backward_kernel(
    second_ref, dy_ref, expand_ref, contract_ref, wo_ref, mixed_ref, resid_ref, bias_ref, params_ref,
    q_ref, kv_ref, wide_ref, lse_ref, first_in_ref, w_ref, x_ref,
    block_out, input_grad_ref, small_out, qkv_out, expand_out, contract_out, output_out,
    act, grad_pre, right, part, near, far, branch, sums_small,
    rows, turned, kv_turned, grad_rows, grad_turned, sums, packed, grad_mine, dq_mine, dkv_mine, dkv_in,
    big, stage, big_last, stage_last, dq_parts, dkv_parts,
    gq, gk, gv, qkv, qkv_stage, norm_send, norm_in, small_steps, small_in,
    swap_send, swap_recv, swap_local, big_local, big_send, big_recv, all_send, all_recv,
    half_send, half_recv, full_send, full_recv, small_send, small_recv, pair_send, pair_recv,
    *team_sems,
):
    place = Place()
    plane, pair, team = Plane(place), Pair(place), Team(place)
    column, cube = Column(place), Cube(place)
    half = query_half(place)
    sequence = place.spot // 4

    def swap(k, group, src, dst):
        return Swap(group, src, dst, swap_send.at[k], swap_recv.at[k], swap_local.at[k])

    def fold(k):
        return Fold(team, part.at[k], near.at[k], far.at[k], team_sems[2 * k], team_sems[2 * k + 1])

    meet([plane, pair, team, column])

    second_fold = fold(0)

    def make(t):
        pre = matmul(second_ref[t], expand_ref[...]) + bias_ref[...]
        value, slope = gelu_both(pre)
        act[t] = value.astype(BF16)
        grad = (matmul_nt(dy_ref[t], contract_ref[...]) * slope).astype(BF16)
        grad_pre[t] = grad
        part[0, t] = matmul_nt(grad, expand_ref[...]).astype(BF16)

    second_fold.send(make)

    def turn(src):
        for t in range(4):
            for at in range(0, src.shape[2], 256):
                right[pl.ds(at, 256), pl.ds(t * 128, 128)] = src[t, :, pl.ds(at, 256)].astype(F32).T.astype(BF16)

    def weight_grad(count, other, put):
        for at in range(0, count, 256):
            left = right[pl.ds(at, 256), :]
            total = matmul(left[:, :128], other[0])
            for t in range(1, 4):
                total = total + matmul(left[:, t * 128 : t * 128 + 128], other[t])
            put(at, total.astype(BF16))

    def bias_grad(row, src):
        total = jnp.sum(src[0].astype(F32), axis=0, keepdims=True)
        for t in range(1, 4):
            total = total + jnp.sum(src[t].astype(F32), axis=0, keepdims=True)
        sums_small[pl.ds(row, 1), :] = total

    halving = Halving(
        big_parts(cube),
        [big.at[k] for k in range(4)] + [big_last],
        [stage.at[k] for k in range(4)] + [stage_last],
        big_send, big_recv,
    )

    def put_contract(at, value):
        big[2 + at // 512, pl.ds(at % 512, 256), :] = value

    def put_expand(at, value):
        big[at // 512, pl.ds(at % 512, 256), :] = value

    def put_output(at, value):
        big_last[pl.ds(0, 256), :] = value[:, :512]
        big_last[pl.ds(256, 256), :] = value[:, 512:]

    turn(act)
    weight_grad(1024, dy_ref, put_contract)
    halving.send(0, (2, 3))
    bias_grad(1, dy_ref)
    bias_grad(2, grad_pre)
    grad_second = second_fold.total()
    gain = params_ref[pl.ds(2, 1), :]
    _, unit, inverse = norm_parts(resid_ref[...], gain, 0.0)
    grad_resid = dy_ref[place.shard].astype(F32) + norm_back(grad_second, unit, inverse, gain)
    sums_small[pl.ds(8, 1), :] = jnp.sum(grad_second * unit, axis=0, keepdims=True)
    sums_small[pl.ds(9, 1), :] = jnp.sum(grad_second, axis=0, keepdims=True)
    branch[place.shard] = grad_resid.astype(BF16)
    share = Share(team, branch, branch.at[place.shard], *team_sems[6:8])
    share.send()
    turn(second_ref)
    weight_grad(1024, grad_pre, put_expand)
    halving.send(0, (0, 1))
    share.forward()
    spread_rows(q_ref, rows, False, 0.125)
    turn_rows(rows, turned, 2048)
    turn_rows(kv_ref, kv_turned, 4096)
    for at in range(0, 4096, TILE):
        sums[pl.ds(at, TILE), :] = jnp.zeros((TILE, 128), F32)
    share.take()
    for t in range(4):
        grad_mixed = matmul_nt(branch[t], wo_ref[...]).astype(BF16)
        for two in range(2):
            lanes = slice(two * 128, two * 128 + 128)
            at = t * 4 + two * 2
            packed[at], packed[at + 1] = swap_heads(grad_mixed[:HALF, lanes], grad_mixed[HALF:, lanes])
    to_heads = swap(0, plane, lambda t: packed.at[t], lambda j, t: grad_mine.at[j])
    to_heads.send_all()
    for t in range(4):
        right[pl.ds(0, 256), pl.ds(t * 128, 128)] = mixed_ref[pl.ds(t * 128, 128), :].astype(F32).T.astype(BF16)
    weight_grad(256, branch, put_output)
    halving.send(0, (4,))
    ffn_fold = fold(1)

    def make_ffn(t):
        part[1, t] = matmul(act[t], contract_ref[...]).astype(BF16)

    ffn_fold.send(make_ffn)
    bias_grad(0, branch)

    dq = swap(1, plane, lambda t: dq_mine.at[t], lambda j, t: dq_parts.at[j])
    dkv = [
        swap(
            2 + k, plane,
            lambda t, k=k: dkv_mine.at[kv_place(half_of(place.layer) * 16 + t, k == 0)],
            lambda j, t, k=k: kv_block(dkv_parts, j, k == 0),
        )
        for k in range(2)
    ]

    def half_of(layer):
        return (layer + place.shard // 2 + sequence // 2) % 2

    def piece_rows(layer, k):
        start = half_of(layer) * 1024
        start = (3072 - start if k >= 2 else start) + (k % 2) * TILE
        return pl.ds(pl.multiple_of(start, TILE), TILE)

    def give(k):
        return pltpu.make_async_remote_copy(
            src_ref=dkv_mine.at[piece_rows(1 - place.layer, k)],
            dst_ref=dkv_in.at[k],
            send_sem=pair_send.at[k],
            recv_sem=pair_recv.at[k],
            device_id=pair.device(1 - place.layer),
            device_id_type=MESH,
        )

    halving.add(0)
    halving.send(1)
    to_heads.take_all()
    spread_rows(grad_mine, grad_rows, True, 1.0)
    turn_rows(grad_rows, grad_turned, 2048)
    for number, tile in enumerate((0, 3, 1, 2)):
        cols = pl.ds(tile * TILE, TILE)
        last = tile_place(half, tile)
        delta = jnp.sum(grad_turned[HALF:, cols].astype(F32) * wide_ref[:, cols], axis=0, keepdims=True)
        lse = lse_ref[:, cols]

        def step(kt, accum, masked):
            kv = kv_ref[key_rows(kt), :]
            scores = matmul(kv, turned[:, cols])
            if masked:
                scores = hide_later(scores)
            probs = jnp.exp(scores - lse)
            grad_probs = matmul(kv, grad_turned[:, cols])
            grad_scores = (probs * (grad_probs - delta)).astype(BF16)
            sums[key_rows(kt), :] += matmul(probs.astype(BF16), grad_rows[cols, :]) + matmul(
                grad_scores, rows[cols, :]
            )
            return accum + matmul(kv_turned[:HALF, key_rows(kt)], grad_scores)

        accum = lax.fori_loop(
            0, last, lambda kt, c: step(kt, c, False), jnp.zeros((HALF, TILE), F32)
        )
        accum = step(last, accum, True)
        pack_rows(accum * 0.125, dq_mine, tile)
        if number < 3:
            halving.add(number + 1)
            halving.send(number + 2)
    for k in range(4):
        theirs = piece_rows(1 - place.layer, k)
        dkv_mine[theirs, :] = sums[theirs, :].astype(BF16)
        give(k).start()
    dq.send_all()
    for k in range(4):
        mine = piece_rows(place.layer, k)
        give(k).wait_recv()
        dkv_mine[mine, :] = (sums[mine, :] + dkv_in[k].astype(F32)).astype(BF16)
        for block in range(8):
            spot = (k % 2) * 8 + block if k < 2 else 15 - ((k % 2) * 8 + block)

            @pl.when(spot != plane.me)
            def _(spot=spot, k=k):
                dkv[k // 2].copy(spot).start()

    for item in dkv:
        item.own().start()
    halving.add(4)
    outs = [expand_out.at[0], expand_out.at[1], contract_out.at[0], contract_out.at[1], output_out]
    gather = Doubling(halving.parts, outs, all_send, all_recv)
    starts = [
        pltpu.make_async_copy(
            piece.view(halving.buffers[k], piece.held[5]), piece.view(outs[k], piece.held[5]), big_local.at[k]
        )
        for k, piece in enumerate(gather.parts)
    ]
    for start in starts:
        start.start()
    block_out[...] = (resid_ref[...] + ffn_fold.total() + params_ref[pl.ds(5, 1), :]).astype(BF16)
    for at in range(0, 1024, 256):
        right[pl.ds(at, 256), :] = first_in_ref[:, pl.ds(at, 256)].astype(F32).T.astype(BF16)
    for start in starts:
        start.wait()
    gather.send(3)

    parts = [Part(cube, 2 * k, 256, 16) for k in range(3)]
    qkv_halving = Halving(
        parts, [qkv.at[k] for k in range(3)], [qkv_stage.at[k] for k in range(3)], half_send, half_recv
    )

    def projection_grad(k, grad):
        for f in range(4):
            qkv[k, :, pl.ds(f * 256, 256)] = matmul(right[pl.ds(f * 256, 256), :], grad[...]).astype(BF16)
        qkv_halving.send(0, (k,))

    dq.take_all()
    unpack_into(gq, dq_parts)
    projection_grad(0, gq)
    for item in dkv:
        item.take_all()
    for at in range(0, 512, 128):
        here = pl.ds(at, 128)
        for two in range(2):
            lanes = pl.ds(two * 128, 128)
            gk[here, lanes], gv[here, lanes] = swap_heads(
                dkv_parts[here, two * 256 : two * 256 + 128], dkv_parts[here, two * 256 + 128 : two * 256 + 256]
            )
    projection_grad(1, gk)
    projection_grad(2, gv)
    first_fold = fold(2)

    def make_first(t):
        here = pl.ds(pl.multiple_of(t * 128, 128), 128)
        part[2, t] = (
            matmul_nt(gq[here, :], w_ref[0])
            + matmul_nt(gk[here, :], w_ref[1])
            + matmul_nt(gv[here, :], w_ref[2])
        ).astype(BF16)

    first_fold.send(make_first)
    for step in range(2):
        gather.take(3 - step)
        gather.send(2 - step)
        qkv_halving.add(step)
        qkv_halving.send(step + 1)
    grad_first = first_fold.total()
    gain = params_ref[pl.ds(0, 1), :]
    _, unit, inverse = norm_parts(x_ref[...].astype(F32), gain, 0.0)
    input_grad_ref[...] = (grad_resid + norm_back(grad_first, unit, inverse, gain)).astype(BF16)
    norm_rows = [
        jnp.sum(grad_first * unit, axis=0, keepdims=True),
        jnp.sum(grad_first, axis=0, keepdims=True),
    ]
    norm_send[...] = jnp.zeros_like(norm_send)
    for t in range(4):
        for k in range(2):
            norm_send[t, pl.ds(k, 1), :] = norm_rows[k][:, t * 256 : t * 256 + 256]
            norm_send[t, pl.ds(2 + k, 1), :] = sums_small[pl.ds(8 + k, 1), pl.ds(t * 256, 256)]
    to_column = swap(4, column, lambda t: norm_send.at[t], lambda j, t: norm_in.at[j])
    to_column.send_all()
    for step in range(2, 5):
        if step == 2:
            gather.take(1)
            gather.send(0)
        qkv_halving.add(step)
        if step < 4:
            qkv_halving.send(step + 1)
    cross = []
    for k, piece in enumerate(parts):
        row, _ = piece.held[5]

        def block(ref, f, row=row):
            return ref.at[
                pl.ds(pl.multiple_of(row, 16), 16), pl.ds(pl.multiple_of(f * 256, 256), 256)
            ]

        cross.append(swap(
            5 + k, column,
            lambda t, k=k, block=block: block(qkv.at[k], t),
            lambda j, t, k=k, block=block: block(qkv_out.at[k], j),
        ))
    for item in cross:
        item.send_all()
    to_column.take_all()
    small = small_steps.at[0]
    small[pl.ds(0, 8), :] = norm_in[0] + norm_in[1] + norm_in[2] + norm_in[3]
    small[pl.ds(4, 1), :] = jnp.sum(gq[...].astype(F32), axis=0, keepdims=True)
    small[pl.ds(5, 1), :] = jnp.sum(gv[...].astype(F32), axis=0, keepdims=True)
    own_lanes = pl.ds(pl.multiple_of(place.shard * 256, 256), 256)
    small[pl.ds(6, 1), :] = sums_small[pl.ds(0, 1), own_lanes]
    small[pl.ds(7, 1), :] = sums_small[pl.ds(1, 1), own_lanes]
    small[pl.ds(8, 8), :] = jnp.zeros((8, 256), F32)
    for t in range(4):
        small[pl.ds(8 + t, 1), :] = sums_small[pl.ds(2, 1), pl.ds(t * 256, 256)]
    full = Doubling(parts, [qkv_out.at[k] for k in range(3)], full_send, full_recv)

    def small_copy(step):
        return pltpu.make_async_remote_copy(
            src_ref=small_steps.at[step],
            dst_ref=small_in.at[step],
            send_sem=small_send.at[step],
            recv_sem=small_recv.at[step],
            device_id=cube.device(step),
            device_id_type=MESH,
        )

    small_copy(0).start()
    for item in cross:
        item.take_all()
    for step in range(5):
        if step > 0:
            full.send(4 - step)
            small_copy(step).start()
            full.take(4 - step)
        small_copy(step).wait_recv()
        small_steps[step + 1] = small_steps[step] + small_in[step]
    small_out[...] = small_steps[5]
    gather.take(0)
    for item in [to_heads, dq, *dkv, to_column, *cross]:
        item.sent_all()
    for item in (second_fold, ffn_fold, first_fold, share):
        item.sent()
    for item in (halving, gather, qkv_halving, full):
        item.finish()
    for k in range(4):
        give(k).wait_send()
    for step in range(5):
        small_copy(step).wait_send()


def backward(*args):
    vmem = pl.BlockSpec(memory_space=pltpu.VMEM)
    anywhere = pl.BlockSpec(memory_space=pl.ANY)
    blocks = pltpu.VMEM((4, 128, 1024), BF16)
    heads = pltpu.VMEM((16, HALF, 128), BF16)
    return pl.pallas_call(
        backward_kernel,
        name="backward",
        out_shape=[
            jax.ShapeDtypeStruct((128, 1024), BF16),
            jax.ShapeDtypeStruct((128, 1024), BF16),
            jax.ShapeDtypeStruct((16, 256), F32),
            jax.ShapeDtypeStruct((3, 256, 1024), BF16),
            jax.ShapeDtypeStruct((2, 512, 1024), BF16),
            jax.ShapeDtypeStruct((2, 512, 1024), BF16),
            jax.ShapeDtypeStruct((512, 512), BF16),
        ],
        in_specs=[vmem] * len(args),
        out_specs=[vmem] * 3 + [anywhere] * 4,
        scratch_shapes=[
            blocks,
            blocks,
            pltpu.VMEM((1024, 512), BF16),
            pltpu.VMEM((3, 4, 128, 1024), BF16),
            pltpu.VMEM((3, 2, 128, 1024), BF16),
            pltpu.VMEM((3, 128, 1024), BF16),
            blocks,
            pltpu.VMEM((16, 1024), F32),
            pltpu.VMEM((2048, 128), BF16),
            pltpu.VMEM((128, 2048), BF16),
            pltpu.VMEM((128, 4096), BF16),
            pltpu.VMEM((2048, 128), BF16),
            pltpu.VMEM((128, 2048), BF16),
            pltpu.VMEM((4096, 128), F32),
            heads,
            heads,
            heads,
            pltpu.VMEM((4096, 128), BF16),
            pltpu.VMEM((4, TILE, 128), BF16),
            pltpu.VMEM((4, 512, 1024), BF16),
            pltpu.VMEM((4, 512, 1024), BF16),
            pltpu.VMEM((512, 512), BF16),
            pltpu.VMEM((512, 512), BF16),
            heads,
            pltpu.VMEM((512, 512), BF16),
            pltpu.VMEM((512, 256), BF16),
            pltpu.VMEM((512, 256), BF16),
            pltpu.VMEM((512, 256), BF16),
            pltpu.VMEM((3, 256, 1024), BF16),
            pltpu.VMEM((3, 256, 1024), BF16),
            pltpu.VMEM((4, 8, 256), F32),
            pltpu.VMEM((4, 8, 256), F32),
            pltpu.VMEM((6, 16, 256), F32),
            pltpu.VMEM((5, 16, 256), F32),
            *swap_sems(8),
            pltpu.SemaphoreType.DMA((5,)),
            *([pltpu.SemaphoreType.DMA((5, 5))] * 4),
            *([pltpu.SemaphoreType.DMA((3, 5))] * 4),
            *([pltpu.SemaphoreType.DMA((5,))] * 2),
            *([pltpu.SemaphoreType.DMA((4,))] * 2),
            *(TEAM_SEMS * 4),
        ],
        compiler_params=pltpu.CompilerParams(
            collective_id=2, has_side_effects=True, vmem_limit_bytes=VMEM_LIMIT
        ),
    )(*args)


def on_device(
    tokens, query_weight, key_weight, value_weight, output_weight, expand_weight, contract_weight,
    query_bias, value_bias, output_bias, expand_bias, contract_bias,
    first_gain, first_shift, second_gain, second_shift, cotangent,
):
    vectors = [
        first_gain, first_shift, second_gain, second_shift, output_bias, contract_bias, query_bias, value_bias
    ]
    vectors = jnp.concatenate(vectors).astype(F32).reshape(8, 256)
    first_in, mixed, resid, wide, lse, params, q_mine, kv_mine, dy_all, second_in, weights = forward(
        vectors, tokens[0], output_weight, cotangent[0], query_weight, key_weight, value_weight
    )
    block_output, input_grad, small, qkv, expand, contract, output = backward(
        second_in, dy_all, expand_weight, contract_weight, output_weight, mixed, resid,
        expand_bias[None].astype(F32), params,
        q_mine, kv_mine, wide, lse, first_in, weights, tokens[0],
    )
    return (
        block_output[None],
        input_grad[None],
        qkv[0].astype(F32),
        qkv[1].astype(F32),
        qkv[2].astype(F32),
        jnp.concatenate([output[:256], output[256:]], axis=1).astype(F32),
        expand.reshape(1024, 1024).astype(F32),
        contract.reshape(1024, 1024).astype(F32),
        small[4],
        small[5],
        small[6],
        small[8:12].reshape(1024),
        small[7],
        small[0],
        small[1],
        small[2],
        small[3],
    )


def solution(mesh):
    weights = [P("fsdp", None)] * 4 + [P(None, "fsdp"), P("fsdp", None)]
    rows = P("fsdp", "seq", None)
    return jax.shard_map(
        on_device,
        mesh=mesh,
        in_specs=(rows, *weights, *([P("fsdp")] * 9), rows),
        out_specs=(rows, rows, *weights, *([P("fsdp")] * 9)),
        check_vma=False,
    )
```
